256 devices in a mesh: pipe: 4 (over y), dp: 32 (over z, x_hi, core), tensor: 2 (over x_lo).
Axes of the slice: x: 4 (x_hi: 2, x_lo: 2; x = x_hi * 2 + x_lo), y: 4, z: 8, core: 2. Of those that a mesh axis runs over, the one named last changes fastest.
Arguments:
- section_out: bfloat16 [4, 4096, 16384], P('pipe', 'dp', 'tensor'), may hold values from -6 to 6
- saved_stream: bfloat16 [4, 4096, 16384], P('pipe', 'dp', 'tensor'), may hold values from -6 to 6
- section_grad: bfloat16 [4, 4096, 16384], P('pipe', 'dp', 'tensor'), may hold values from -0.59765625 to 0.59765625
- key_grad: bfloat16 [4, 4096, 512], P('pipe', ('dp', 'tensor')), may hold values from -3 to 3
- key_weight: bfloat16 [4, 16384, 512], P('pipe', 'tensor'), may hold values from -0.09375 to 0.09375
- adapter_in: bfloat16 [4, 16384, 64], P('pipe', 'tensor'), may hold values from -0.046875 to 0.046875
- adapter_out: bfloat16 [4, 64, 512], P('pipe'), may hold values from -0.75 to 0.75
- magnitude: float32 [4, 512], P('pipe'), may hold values from 0.5 to 2
Outputs:
- projected_keys: bfloat16 [4, 4096, 512], P('pipe', ('dp', 'tensor'))
- stream_grad: bfloat16 [4, 4096, 16384], P('pipe', 'dp', 'tensor')
- magnitude_grad: float32 [4, 512], P('pipe')
- adapter_out_grad: float32 [4, 64, 512], P('pipe', None, 'dp')
- adapter_in_grad: float32 [4, 16384, 64], P('pipe', ('tensor', 'dp'))
The draws below stay inside these ranges and needn't reach their ends.
All inputs are finite; a program needn't handle non-finite values.
Results may differ from the reference program's by a relative error of at most 0.0041.
Values may be sent and summed in bfloat16 or wider, within the bound.
A program may use at most 128 MiB of HBM per device.

```python
import math
import jax
import jax.numpy as jnp
from jax import lax

D = 16384
KV_COLS = 512
RANK = 64
SECTIONS = 4
TOKENS = 4096
REPLICAS = 32


def rising_rows(rise_factor):
    position = jnp.arange(D, dtype=jnp.float32) / D
    mean_square = (rise_factor - 1.0) / math.log(rise_factor)
    return jnp.exp(0.5 * math.log(rise_factor) * position) / math.sqrt(mean_square)


def draw_key_weight(key, part):
    key = jax.random.fold_in(key, 11)
    shape = (SECTIONS, D, KV_COLS)
    entries = jnp.clip(jax.random.normal(key, shape, jnp.float32), -6.0, 6.0)
    row_scale = rising_rows(16.0)
    values = entries * row_scale[None, :, None] / math.sqrt(D)
    return values.astype(jnp.bfloat16)


def steps_of(own_key, extent, split, low, largest):
    loudness, own = 1.0, jax.random.fold_in(own_key, 6)
    for axis_at, blocks in split:
        heights = jnp.exp(jax.random.uniform(jax.random.fold_in(own, axis_at), (blocks,), jnp.float32, low / len(split), largest / len(split)))
        loudness = loudness * jnp.repeat(heights, extent[axis_at] // blocks).reshape([-1 if axis == axis_at else 1 for axis in range(len(extent))])
    return loudness


def normal_values(key, dims, spread, bound, split=(), kind=jnp.bfloat16):
    values = spread * jax.random.normal(key, dims, jnp.float32)
    if split:
        values = values * steps_of(key, dims, split, -0.22, 0.18)
    return jnp.clip(values, -bound, bound).astype(kind)


def setup_inputs(seed: int = 0) -> dict:
    key_of = jax.random.split(jax.random.key(seed), 9)
    return {
        "section_out": normal_values(key_of[0], (SECTIONS, TOKENS, D), 1.0, 6.0, ((0, 4), (1, 32), (2, 2))),
        "saved_stream": normal_values(key_of[1], (SECTIONS, TOKENS, D), 1.0, 6.0, ((0, 4), (1, 32), (2, 2))),
        "section_grad": normal_values(key_of[2], (SECTIONS, TOKENS, D), 0.1, 0.59765625, ((0, 4), (1, 32), (2, 2))),
        "key_grad": normal_values(key_of[3], (SECTIONS, TOKENS, KV_COLS), 0.5, 3.0, ((0, 4), (1, 64))),
        "key_weight": draw_key_weight(jax.random.fold_in(key_of[8], 71), 0),
        "adapter_in": normal_values(key_of[5], (SECTIONS, D, RANK), D ** -0.5, 0.046875, ((0, 4), (1, 2))),
        "adapter_out": normal_values(key_of[6], (SECTIONS, RANK, KV_COLS), RANK ** -0.5, 0.75, ((0, 4),)),
        "magnitude": jnp.clip(jnp.exp(math.log(2.0) - 1.3862944 * jax.random.uniform(key_of[7], (SECTIONS, KV_COLS), jnp.float32) ** steps_of(key_of[7], (SECTIONS, KV_COLS), ((0, 4),), -0.2, 0.2)), 0.5, 2.0),
    }


EPSILON = 1e-06
HIGHEST_MODE = lax.Precision.HIGHEST

def contract_rows(left_side, right_side, precision_mode=None):
    return lax.dot_general(left_side, right_side, (((0,), (0,)), ((), ())), precision=precision_mode, preferred_element_type=jnp.float32)

def contract_cols(left_side, right_side, precision_mode=None):
    return lax.dot_general(left_side, right_side, (((1,), (1,)), ((), ())), precision=precision_mode, preferred_element_type=jnp.float32)

def project(stream, weight, adapt_in, up_wide):
    low_part = jnp.dot(stream, adapt_in, preferred_element_type=jnp.float32)
    raw_part = jnp.dot(stream, weight, preferred_element_type=jnp.float32) + jnp.dot(low_part, up_wide, precision=HIGHEST_MODE)
    return (raw_part, low_part)

def one_section(inputs):
    forward_stream, saved_rows, next_grad, key_cot, weight, adapt_in, adapt_out, magnitudes = inputs
    up_wide = adapt_out.astype(jnp.float32)
    combined = weight.astype(jnp.float32) + jnp.dot(adapt_in, adapt_out, preferred_element_type=jnp.float32)
    col_norm = jnp.sqrt(lax.optimization_barrier(jnp.sum(combined * combined, axis=0)) + EPSILON)
    col_scale = magnitudes / col_norm
    raw_keys, unused_low = project(forward_stream, weight, adapt_in, up_wide)
    key_out = (raw_keys * col_scale).astype(jnp.bfloat16)
    key_scaled = key_cot.astype(jnp.float32) * col_scale
    key_scaled_b = key_scaled.astype(jnp.bfloat16)
    low_grad = contract_cols(key_scaled, up_wide, HIGHEST_MODE).astype(jnp.bfloat16)
    stream_part = contract_cols(key_scaled_b, weight) + contract_cols(low_grad, adapt_in)
    stream_out = (next_grad.astype(jnp.float32) + stream_part).astype(jnp.bfloat16)
    raw_saved, low_saved = project(saved_rows, weight, adapt_in, up_wide)
    scale_grad = lax.optimization_barrier(jnp.sum(key_cot.astype(jnp.float32) * raw_saved, axis=0))
    out_direct = contract_rows(low_saved, key_scaled, HIGHEST_MODE)
    in_direct = contract_rows(saved_rows, low_grad)
    factor = -scale_grad * magnitudes / (col_norm * col_norm * col_norm)
    cross = contract_rows(adapt_in.astype(jnp.float32), combined, HIGHEST_MODE)
    mag_grad = scale_grad / col_norm / REPLICAS
    out_grad = (out_direct + cross * factor) / REPLICAS
    turned = factor[:, None] * up_wide.T
    in_grad = (in_direct + jnp.dot(combined, turned, precision=HIGHEST_MODE)) / REPLICAS
    return (key_out, stream_out, mag_grad, out_grad, in_grad)

def reference(section_out, saved_stream, section_grad, key_grad, key_weight, adapter_in, adapter_out, magnitude):
    forward_stream = jnp.roll(section_out, 1, axis=0)
    next_grad = jnp.roll(section_grad, -1, axis=0)
    return lax.map(one_section, (forward_stream, saved_stream, next_grad, key_grad, key_weight, adapter_in, adapter_out, magnitude))
```

```python
import jax
import jax.numpy as jnp
from jax import lax
from jax.experimental import pallas as pl
from jax.experimental.pallas import tpu as pltpu
from jax.sharding import PartitionSpec as P

EPSILON = 1e-06
MESH = pl.DeviceIdType.MESH
BF = jnp.bfloat16
F32 = jnp.float32

PIPES = 4
REPLICAS = 32
RINGS = 8
TOK = 128
HALF = 64
COLS = 512
RANK = 64
FEAT = 8192
SHARE = FEAT // REPLICAS
OUTROWS = COLS // REPLICAS
DEPTH = 512
FWD_PIECES = 4
GRAD_PIECES = 8


def mm(left, right, left_dim, right_dim):
    return lax.dot_general(
        left, right, (((left_dim,), (right_dim,)), ((), ())), preferred_element_type=F32
    )


def halves(value):
    upper = value.astype(BF)
    lower = (value - upper.astype(F32)).astype(BF)
    return upper, lower


def mm2(wide, narrow, left_dim, right_dim):
    upper, lower = halves(wide)
    return mm(upper, narrow, left_dim, right_dim) + mm(lower, narrow, left_dim, right_dim)


def kernel(
    x, sv, sg, kg, w, bt, a, mag,
    keys, so, mg, og, ig,
    wv, lv, fw, gr, st, sp, kc, raw, low, sq, sqr, ksb, lgv, fac, flo,
    ox, oxr, o2, o2r, o3, o3r, o4, o4r,
    s0, s0r, s1, s1r, zs, s3, s3r,
    ind, ra, sb, rb, c0, rc, fp, fpr, cv,
    loc, outs, fs, fr, gs, gf, ts, tr, cs, cr, zsd, zrv, hs, hr,
):
    p = lax.axis_index("pipe")
    d = lax.axis_index("dp")
    t = lax.axis_index("tensor")
    z, h, c = d // 4, (d // 2) % 2, d % 2

    def dev(p_=p, z_=z, h_=h, c_=c, t_=t):
        return {"pipe": p_, "dp": (z_ * 2 + h_) * 2 + c_, "tensor": t_}

    up, down = dev(p_=(p + 1) % PIPES), dev(p_=(p + PIPES - 1) % PIPES)
    pair, mate, across = dev(t_=1 - t), dev(c_=1 - c), dev(h_=1 - h)
    ring = [dev(z_=(z + k) % RINGS) for k in range(1, RINGS)]

    def remote(src, dst, ssem, rsem, to):
        cp = pltpu.make_async_remote_copy(
            src_ref=src, dst_ref=dst, send_sem=ssem, recv_sem=rsem, device_id=to, device_id_type=MESH
        )
        cp.start()
        return cp

    locals_ = [
        pltpu.make_async_copy(kg, kc.at[t], loc.at[0]),
        pltpu.make_async_copy(sv, lv.at[pl.ds(0, TOK)], loc.at[1]),
        pltpu.make_async_copy(bt, lv.at[pl.ds(TOK, RANK)], loc.at[2]),
    ]
    for i in range(4):
        rows = pl.ds(i * (FEAT // 4), FEAT // 4)
        locals_.append(pltpu.make_async_copy(w.at[rows], wv.at[rows], loc.at[3 + i]))
    for cp in locals_:
        cp.start()

    barrier = pltpu.get_barrier_semaphore()
    peers = [up, down, pair, mate, across] + ring
    for to in peers:
        pl.semaphore_signal(barrier, inc=1, device_id=to, device_id_type=MESH)
    pl.semaphore_wait(barrier, len(peers))

    kcp = remote(kg, kc.at[t], ts.at[0], tr.at[0], pair)
    fwd, grad = [], []
    wide = FEAT // FWD_PIECES
    narrow = FEAT // GRAD_PIECES
    for i in range(GRAD_PIECES):
        j = i % FWD_PIECES
        rows = pl.ds(pl.multiple_of((1 - t if i < FWD_PIECES else t) * HALF, HALF), HALF)
        at = (rows, pl.ds(j * wide, wide))
        fwd.append(remote(x.at[at], fw.at[at], fs.at[i], fr.at[i], up))
        at = (slice(None), pl.ds(i * narrow, narrow))
        grad.append(remote(sg.at[at], gr.at[at], gs.at[i], gf.at[i], down))

    raw[...] = jnp.zeros_like(raw)
    low[...] = jnp.zeros_like(low)
    sq[...] = jnp.zeros_like(sq)
    for cp in locals_:
        cp.wait()

    @pl.loop(0, FEAT // DEPTH)
    def _(i):
        part = pl.ds(pl.multiple_of(i * DEPTH, DEPTH), DEPTH)
        left = lv[:, part]
        wc = wv[part, :]
        bc = lv[pl.ds(TOK, RANK), part]
        raw[...] += mm(left, wc, 1, 0)
        low[...] += mm(left, bc, 1, 1)
        combined = wc.astype(F32) + mm(bc, a[...], 0, 0)
        sq[...] += jnp.sum((combined * combined).reshape(DEPTH // 8, 8, COLS), axis=0)

    sqc = remote(sq, sqr, ts.at[1], tr.at[1], pair)

    av = a[...]
    lows = low[pl.ds(0, TOK), :]
    lhi, llo = halves(lows)
    raw_saved = raw[pl.ds(0, TOK), :] + mm(lhi, av, 1, 0) + mm(llo, av, 1, 0)
    kcp.wait_recv()
    cot = kc[...].reshape(TOK, COLS)
    cot32 = cot.astype(F32)
    s0[...] = jnp.sum((cot32 * raw_saved).reshape(TOK // 8, 8, COLS), axis=0)
    s0c = remote(s0, s0r, ts.at[2], tr.at[2], pair)
    ox[:, pl.ds(0, RANK)] = mm(cot, lhi, 0, 0) + mm(cot, llo, 0, 0)
    cross = raw[pl.ds(TOK, RANK), :] + mm2(low[pl.ds(TOK, RANK), :], av, 1, 0)
    ox[:, pl.ds(RANK, RANK)] = cross.T
    oxc = remote(ox, oxr, ts.at[3], tr.at[3], pair)

    sqc.wait_recv()
    norm = jnp.sqrt(jnp.sum(sq[...] + sqr[...], axis=0, keepdims=True) + EPSILON)
    scale = mag[...] / norm
    scaled = cot32 * scale
    shi, slo = halves(scaled)
    ksb[...] = shi
    low_grad = mm(shi, av, 1, 1) + mm(slo, av, 1, 1)
    lgv[...] = low_grad.astype(BF)
    turned_grad = low_grad.T.astype(BF)

    @pl.loop(0, REPLICAS // 2)
    def _(i):
        for k in range(2):
            part = pl.ds(pl.multiple_of((i * 2 + k) * SHARE, SHARE), SHARE)
            ind[k, i] = mm(turned_grad, lv[pl.ds(0, TOK), part], 1, 0)

    indc = remote(ind.at[1 - c], ra, cs.at[0], cr.at[0], mate)

    s0c.wait_recv()
    s1[...] = s0[...] + s0r[...]
    s1c = remote(s1, s1r, cs.at[1], cr.at[1], mate)
    oxc.wait_recv()
    both = (ox[...] + oxr[...]).reshape(REPLICAS // 2, 2, OUTROWS, 2 * RANK)
    o2[0] = both[:, 0]
    o2[1] = both[:, 1]
    o2c = remote(o2.at[1 - c], o2r, cs.at[2], cr.at[2], mate)

    def stream_piece(i):
        part = pl.ds(pl.multiple_of(i * narrow, narrow), narrow)
        sp[:, part] = mm(ksb[...], wv[part, :], 1, 1) + mm(lgv[...], lv[pl.ds(TOK, RANK), part], 1, 0)

    pl.loop(0, GRAD_PIECES // 2)(stream_piece)

    s1c.wait_recv()
    zs[z] = s1[...] + s1r[...]
    zsc = [remote(zs.at[z], zs.at[z], zsd.at[k], zrv.at[k], to) for k, to in enumerate(ring)]
    o2c.wait_recv()
    o3[...] = (o2[c] + o2r[...]).reshape(RINGS, 2, OUTROWS, 2 * RANK)
    o3c = [
        remote(o3.at[(z + k + 1) % RINGS], o3r.at[z], zsd.at[7 + k], zrv.at[7 + k], to)
        for k, to in enumerate(ring)
    ]
    indc.wait_recv()

    @pl.loop(0, RINGS)
    def _(i):
        for k in range(2):
            sb[i, k] = (ind[c, i * 2 + k] + ra[i * 2 + k]).astype(BF)

    sbc = [
        remote(sb.at[(z + k + 1) % RINGS], rb.at[z], zsd.at[14 + k], zrv.at[14 + k], to)
        for k, to in enumerate(ring)
    ]

    pl.loop(GRAD_PIECES // 2, GRAD_PIECES)(stream_piece)

    writes = []

    def finish_grad(i):
        grad[i].wait_recv()
        at = (slice(None), pl.ds(i * narrow, narrow))
        st[at] = (sp[at] + gr[at].astype(F32)).astype(BF)
        cp = pltpu.make_async_copy(st.at[at], so.at[at], outs.at[i])
        cp.start()
        writes.append(cp)

    def take_forward(i):
        fwd[i].wait_recv()
        j = i % FWD_PIECES
        rows = pl.ds(pl.multiple_of((1 - t if i < FWD_PIECES else t) * HALF, HALF), HALF)
        if j == 0:
            fac[...] = jnp.zeros_like(fac)
            flo[...] = jnp.zeros_like(flo)

        @pl.loop(0, wide // DEPTH)
        def _(k):
            part = pl.ds(pl.multiple_of(j * wide + k * DEPTH, DEPTH), DEPTH)
            rowsv = fw[rows, part]
            fac[...] += mm(rowsv, wv[part, :], 1, 0)
            flo[...] += mm(rowsv, lv[pl.ds(TOK, RANK), part], 1, 1)

    def partial_keys():
        return fac[...] + mm2(flo[...], a[...], 1, 0)

    for i in range(FWD_PIECES):
        take_forward(i)
        finish_grad(i)
    fp[...] = partial_keys()
    fpc = remote(fp, fpr, ts.at[4], tr.at[4], pair)

    for cp in zsc:
        cp.wait_recv()
    total = zs[0]
    for k in range(1, RINGS):
        total = total + zs[k]
    s3[...] = total
    s3c = remote(s3, s3r, hs.at[0], hr.at[0], across)
    for cp in o3c:
        cp.wait_recv()
    total = o3[z]
    for k in range(1, RINGS):
        total = total + o3r[(z + k) % RINGS]
    o4[...] = total
    o4c = remote(o4.at[1 - h], o4r, hs.at[1], hr.at[1], across)

    take_forward(4)
    finish_grad(4)
    for cp in sbc:
        cp.wait_recv()
    for k in range(2):
        total = ind[c, z * 2 + k] + ra[z * 2 + k]
        for n in range(1, RINGS):
            total = total + rb[(z + n) % RINGS, k].astype(F32)
        c0[k] = total
    c0c = remote(c0.at[1 - h], rc, hs.at[2], hr.at[2], across)

    take_forward(5)
    finish_grad(5)
    s3c.wait_recv()
    scale_grad = jnp.sum(s3[...] + s3r[...], axis=0, keepdims=True)
    factor = -scale_grad * mag[...] / (norm * norm * norm)
    mg[...] = scale_grad / norm / REPLICAS
    columns = jnp.concatenate([scale, factor, jnp.zeros((6, COLS), F32)], axis=0)
    cv[...] = columns.T
    o4c.wait_recv()
    mine = pl.ds(pl.multiple_of(d * OUTROWS, OUTROWS), OUTROWS)
    direct = o4[h][:, :RANK] + o4r[:, pl.ds(0, RANK)]
    shared = o2[c, z * 2 + h][:, RANK:]
    og[...] = (direct * cv[mine, pl.ds(0, 1)] + shared * cv[mine, pl.ds(1, 1)]) / REPLICAS
    turned = a[...].astype(F32) * factor
    thi, tlo = halves(turned)
    part = pl.ds(pl.multiple_of(d * SHARE, SHARE), SHARE)
    wsh = wv[part, :]
    small = mm(thi, a[...], 1, 1) + mm(tlo, a[...], 1, 1)
    term = mm(thi, wsh, 1, 1) + mm(tlo, wsh, 1, 1) + mm2(small, lv[pl.ds(TOK, RANK), part], 1, 0)

    take_forward(6)
    finish_grad(6)
    c0c.wait_recv()
    ig[...] = (c0[h] + rc[...] + term) / REPLICAS
    fpc.wait_recv()

    take_forward(7)
    keys[...] = ((partial_keys() + fpr[...]) * scale).astype(BF)
    finish_grad(7)

    for cp in [kcp, sqc, s0c, oxc, indc, s1c, o2c, fpc, s3c, o4c, c0c] + zsc + o3c + sbc + fwd + grad:
        cp.wait_send()
    for cp in writes:
        cp.wait()


def per_device(section_out, saved_stream, section_grad, key_grad, key_weight, adapter_in, adapter_out, magnitude):
    vmem = pl.BlockSpec(memory_space=pltpu.VMEM)
    hbm = pl.BlockSpec(memory_space=pl.ANY)
    dma = pltpu.SemaphoreType.DMA
    V = pltpu.VMEM
    half = REPLICAS // 2
    keys, so, mg, og, ig = pl.pallas_call(
        kernel,
        out_shape=[
            jax.ShapeDtypeStruct((HALF, COLS), BF),
            jax.ShapeDtypeStruct((TOK, FEAT), BF),
            jax.ShapeDtypeStruct((1, COLS), F32),
            jax.ShapeDtypeStruct((OUTROWS, RANK), F32),
            jax.ShapeDtypeStruct((RANK, SHARE), F32),
        ],
        in_specs=[hbm] * 6 + [vmem] * 2,
        out_specs=[vmem, hbm, vmem, vmem, vmem],
        scratch_shapes=[
            V((FEAT, COLS), BF),
            V((TOK + RANK, FEAT), BF),
            V((TOK, FEAT), BF),
            V((TOK, FEAT), BF),
            V((TOK, FEAT), BF),
            V((TOK, FEAT), F32),
            V((2, HALF, COLS), BF),
            V((TOK + RANK, COLS), F32),
            V((TOK + RANK, RANK), F32),
            V((8, COLS), F32),
            V((8, COLS), F32),
            V((TOK, COLS), BF),
            V((TOK, RANK), BF),
            V((HALF, COLS), F32),
            V((HALF, RANK), F32),
            V((COLS, 2 * RANK), F32),
            V((COLS, 2 * RANK), F32),
            V((2, half, OUTROWS, 2 * RANK), F32),
            V((half, OUTROWS, 2 * RANK), F32),
            V((RINGS, 2, OUTROWS, 2 * RANK), F32),
            V((RINGS, 2, OUTROWS, 2 * RANK), F32),
            V((2, OUTROWS, 2 * RANK), F32),
            V((OUTROWS, 2 * RANK), F32),
            V((8, COLS), F32),
            V((8, COLS), F32),
            V((8, COLS), F32),
            V((8, COLS), F32),
            V((RINGS, 8, COLS), F32),
            V((8, COLS), F32),
            V((8, COLS), F32),
            V((2, half, RANK, SHARE), F32),
            V((half, RANK, SHARE), F32),
            V((RINGS, 2, RANK, SHARE), BF),
            V((RINGS, 2, RANK, SHARE), BF),
            V((2, RANK, SHARE), F32),
            V((RANK, SHARE), F32),
            V((HALF, COLS), F32),
            V((HALF, COLS), F32),
            V((COLS, 8), F32),
            dma((7,)),
            dma((GRAD_PIECES,)),
            dma((GRAD_PIECES,)),
            dma((GRAD_PIECES,)),
            dma((GRAD_PIECES,)),
            dma((GRAD_PIECES,)),
            dma((5,)),
            dma((5,)),
            dma((3,)),
            dma((3,)),
            dma((21,)),
            dma((21,)),
            dma((3,)),
            dma((3,)),
        ],
        compiler_params=pltpu.CompilerParams(
            collective_id=0, has_side_effects=True, vmem_limit_bytes=56 * 2**20
        ),
        name="relay_tick",
    )(
        section_out[0],
        saved_stream[0],
        section_grad[0],
        key_grad[0],
        key_weight[0],
        adapter_in[0].T,
        adapter_out[0],
        magnitude,
    )
    return (keys[None], so[None], mg, og.T[None], ig.T[None])


def solution(mesh):
    placed = (
        P("pipe", "dp", "tensor"),
        P("pipe", "dp", "tensor"),
        P("pipe", "dp", "tensor"),
        P("pipe", ("dp", "tensor"), None),
        P("pipe", "tensor", None),
        P("pipe", "tensor", None),
        P("pipe", None, None),
        P("pipe", None),
    )
    return jax.shard_map(
        per_device,
        mesh=mesh,
        in_specs=placed,
        out_specs=(
            P("pipe", ("dp", "tensor"), None),
            P("pipe", "dp", "tensor"),
            P("pipe", None),
            P("pipe", None, "dp"),
            P("pipe", ("tensor", "dp"), None),
        ),
        check_vma=False,
    )
```

```python
import jax
import jax.numpy as jnp
from jax import lax
from jax.experimental import pallas as pl
from jax.experimental.pallas import tpu as pltpu
from jax.sharding import PartitionSpec as P

EPSILON = 1e-06
MESH = pl.DeviceIdType.MESH
BF = jnp.bfloat16
F32 = jnp.float32

PIPES = 4
REPLICAS = 32
RINGS = 8
TOK = 128
HALF = 64
COLS = 512
RANK = 64
FEAT = 8192
SHARE = FEAT // REPLICAS
OUTROWS = COLS // REPLICAS
DEPTH = 512
FWD_PIECES = 4
GRAD_PIECES = 8


def mm(left, right, left_dim, right_dim):
    return lax.dot_general(
        left, right, (((left_dim,), (right_dim,)), ((), ())), preferred_element_type=F32
    )


def halves(value):
    upper = value.astype(BF)
    lower = (value - upper.astype(F32)).astype(BF)
    return upper, lower


def mm2(wide, narrow, left_dim, right_dim):
    upper, lower = halves(wide)
    return mm(upper, narrow, left_dim, right_dim) + mm(lower, narrow, left_dim, right_dim)


def kernel(
    x, sv, sg, kg, w, bt, a_in, mag_in,
    keys, so, mg, og, ig,
    a, mag, wv, lv, fw, gr, sp, kc, raw, low, sq, sqr, ksb, lgv, fac, flo,
    ox, oxr, o2, o2r, o3, o3r, o4, o4r,
    s0, s0r, s1, s1r, zs, s3, s3r,
    ind, ra, sb, rb, c0, rc, fp, fpr, cv,
    loc, fs, fr, gs, gf, ts, tr, cs, cr, zsd, zrv, hs, hr, know,
):
    p = lax.axis_index("pipe")
    d = lax.axis_index("dp")
    t = lax.axis_index("tensor")
    z, h, c = d // 4, (d // 2) % 2, d % 2

    def dev(p_=p, z_=z, h_=h, c_=c, t_=t):
        return {"pipe": p_, "dp": (z_ * 2 + h_) * 2 + c_, "tensor": t_}

    up, down = dev(p_=(p + 1) % PIPES), dev(p_=(p + PIPES - 1) % PIPES)
    pair, mate, across = dev(t_=1 - t), dev(c_=1 - c), dev(h_=1 - h)
    ring = [dev(z_=(z + k) % RINGS) for k in range(1, RINGS)]

    def remote(src, dst, ssem, rsem, to):
        cp = pltpu.make_async_remote_copy(
            src_ref=src, dst_ref=dst, send_sem=ssem, recv_sem=rsem, device_id=to, device_id_type=MESH
        )
        cp.start()
        return cp

    locals_ = [
        pltpu.make_async_copy(kg, kc.at[t], loc.at[0]),
        pltpu.make_async_copy(sv, lv.at[pl.ds(0, TOK)], loc.at[1]),
        pltpu.make_async_copy(bt, lv.at[pl.ds(TOK, RANK)], loc.at[2]),
    ]
    locals_.append(pltpu.make_async_copy(a_in, a, loc.at[7]))
    locals_.append(pltpu.make_async_copy(mag_in, mag, loc.at[8]))
    for i in range(4):
        rows = pl.ds(i * (FEAT // 4), FEAT // 4)
        locals_.append(pltpu.make_async_copy(w.at[rows], wv.at[rows], loc.at[3 + i]))
    for cp in locals_:
        cp.start()

    def signal(sem, to):
        pl.semaphore_signal(sem, inc=1, device_id=to, device_id_type=MESH)

    def meet(sem, step):
        @pl.when(z >= step)
        def _():
            signal(sem, dev(z_=z - step))

        @pl.when(z + step < RINGS)
        def _():
            signal(sem, dev(z_=z + step))

    def met(step):
        return jnp.where(z >= step, 1, 0) + jnp.where(z + step < RINGS, 1, 0)

    barrier = pltpu.get_barrier_semaphore()
    near = [up, down, pair, mate, across]
    for to in near:
        signal(barrier, to)
    meet(barrier, 1)
    pl.semaphore_wait(barrier, len(near) + met(1))

    kcp = remote(kg, kc.at[t], ts.at[0], tr.at[0], pair)
    fwd, grad = [], []
    wide = FEAT // FWD_PIECES
    narrow = FEAT // GRAD_PIECES
    for i in range(GRAD_PIECES):
        j = i % FWD_PIECES
        rows = pl.ds(pl.multiple_of((1 - t if i < FWD_PIECES else t) * HALF, HALF), HALF)
        at = (rows, pl.ds(j * wide, wide))
        fwd.append(remote(x.at[at], fw.at[at], fs.at[i], fr.at[i], up))
        at = (slice(None), pl.ds(i * narrow, narrow))
        grad.append(remote(sg.at[at], gr.at[at], gs.at[i], gf.at[i], down))

    meet(know.at[0], 1)

    raw[...] = jnp.zeros_like(raw)
    low[...] = jnp.zeros_like(low)
    sq[...] = jnp.zeros_like(sq)
    for cp in locals_:
        cp.wait()
    pl.semaphore_wait(know.at[0], met(1))
    meet(know.at[1], 2)

    @pl.loop(0, FEAT // DEPTH)
    def _(i):
        part = pl.ds(pl.multiple_of(i * DEPTH, DEPTH), DEPTH)
        left = lv[:, part]
        wc = wv[part, :]
        bc = lv[pl.ds(TOK, RANK), part]
        raw[...] += mm(left, wc, 1, 0)
        low[...] += mm(left, bc, 1, 1)
        combined = wc.astype(F32) + mm(bc, a[...], 0, 0)
        sq[...] += jnp.sum((combined * combined).reshape(DEPTH // 8, 8, COLS), axis=0)

    sqc = remote(sq, sqr, ts.at[1], tr.at[1], pair)
    pl.semaphore_wait(know.at[1], met(2))
    meet(know.at[2], 4)

    av = a[...]
    lows = low[pl.ds(0, TOK), :]
    lhi, llo = halves(lows)
    raw_saved = raw[pl.ds(0, TOK), :] + mm(lhi, av, 1, 0) + mm(llo, av, 1, 0)
    kcp.wait_recv()
    cot = kc[...].reshape(TOK, COLS)
    cot32 = cot.astype(F32)
    s0[...] = jnp.sum((cot32 * raw_saved).reshape(TOK // 8, 8, COLS), axis=0)
    s0c = remote(s0, s0r, ts.at[2], tr.at[2], pair)
    ox[:, pl.ds(0, RANK)] = mm(cot, lhi, 0, 0) + mm(cot, llo, 0, 0)
    cross = raw[pl.ds(TOK, RANK), :] + mm2(low[pl.ds(TOK, RANK), :], av, 1, 0)
    ox[:, pl.ds(RANK, RANK)] = cross.T
    oxc = remote(ox, oxr, ts.at[3], tr.at[3], pair)

    sqc.wait_recv()
    norm = jnp.sqrt(jnp.sum(sq[...] + sqr[...], axis=0, keepdims=True) + EPSILON)
    scale = mag[...] / norm
    scaled = cot32 * scale
    shi, slo = halves(scaled)
    ksb[...] = shi
    low_grad = mm(shi, av, 1, 1) + mm(slo, av, 1, 1)
    lgv[...] = low_grad.astype(BF)
    turned_grad = low_grad.T.astype(BF)

    @pl.loop(0, REPLICAS // 2)
    def _(i):
        for k in range(2):
            part = pl.ds(pl.multiple_of((i * 2 + k) * SHARE, SHARE), SHARE)
            ind[k, i] = mm(turned_grad, lv[pl.ds(0, TOK), part], 1, 0)

    indc = remote(ind.at[1 - c], ra, cs.at[0], cr.at[0], mate)

    s0c.wait_recv()
    s1[...] = s0[...] + s0r[...]
    s1c = remote(s1, s1r, cs.at[1], cr.at[1], mate)
    oxc.wait_recv()
    both = (ox[...] + oxr[...]).reshape(REPLICAS // 2, 2, OUTROWS, 2 * RANK)
    o2[0] = both[:, 0]
    o2[1] = both[:, 1]
    o2c = remote(o2.at[1 - c], o2r, cs.at[2], cr.at[2], mate)

    def stream_piece(i):
        part = pl.ds(pl.multiple_of(i * narrow, narrow), narrow)
        sp[:, part] = mm(ksb[...], wv[part, :], 1, 1) + mm(lgv[...], lv[pl.ds(TOK, RANK), part], 1, 0)

    pl.loop(0, GRAD_PIECES // 2)(stream_piece)

    pl.semaphore_wait(know.at[2], met(4))
    s1c.wait_recv()
    zs[z] = s1[...] + s1r[...]
    zsc = [remote(zs.at[z], zs.at[z], zsd.at[k], zrv.at[k], to) for k, to in enumerate(ring)]
    o2c.wait_recv()
    o3[...] = (o2[c] + o2r[...]).reshape(RINGS, 2, OUTROWS, 2 * RANK)
    o3c = [
        remote(o3.at[(z + k + 1) % RINGS], o3r.at[z], zsd.at[7 + k], zrv.at[7 + k], to)
        for k, to in enumerate(ring)
    ]
    indc.wait_recv()

    @pl.loop(0, RINGS)
    def _(i):
        for k in range(2):
            sb[i, k] = (ind[c, i * 2 + k] + ra[i * 2 + k]).astype(BF)

    sbc = [
        remote(sb.at[(z + k + 1) % RINGS], rb.at[z], zsd.at[14 + k], zrv.at[14 + k], to)
        for k, to in enumerate(ring)
    ]

    pl.loop(GRAD_PIECES // 2, GRAD_PIECES)(stream_piece)

    def finish_grad(i):
        grad[i].wait_recv()
        at = (slice(None), pl.ds(i * narrow, narrow))
        so[at] = (sp[at] + gr[at].astype(F32)).astype(BF)

    def take_forward(i):
        fwd[i].wait_recv()
        j = i % FWD_PIECES
        rows = pl.ds(pl.multiple_of((1 - t if i < FWD_PIECES else t) * HALF, HALF), HALF)
        if j == 0:
            fac[...] = jnp.zeros_like(fac)
            flo[...] = jnp.zeros_like(flo)

        @pl.loop(0, wide // DEPTH)
        def _(k):
            part = pl.ds(pl.multiple_of(j * wide + k * DEPTH, DEPTH), DEPTH)
            rowsv = fw[rows, part]
            fac[...] += mm(rowsv, wv[part, :], 1, 0)
            flo[...] += mm(rowsv, lv[pl.ds(TOK, RANK), part], 1, 1)

    def partial_keys():
        return fac[...] + mm2(flo[...], a[...], 1, 0)

    for i in range(FWD_PIECES):
        take_forward(i)
        finish_grad(i)
    fp[...] = partial_keys()
    fpc = remote(fp, fpr, ts.at[4], tr.at[4], pair)

    for cp in zsc:
        cp.wait_recv()
    total = zs[0]
    for k in range(1, RINGS):
        total = total + zs[k]
    s3[...] = total
    s3c = remote(s3, s3r, hs.at[0], hr.at[0], across)
    for cp in o3c:
        cp.wait_recv()
    total = o3[z]
    for k in range(1, RINGS):
        total = total + o3r[(z + k) % RINGS]
    o4[...] = total
    o4c = remote(o4.at[1 - h], o4r, hs.at[1], hr.at[1], across)

    take_forward(4)
    finish_grad(4)
    for cp in sbc:
        cp.wait_recv()
    for k in range(2):
        total = ind[c, z * 2 + k] + ra[z * 2 + k]
        for n in range(1, RINGS):
            total = total + rb[(z + n) % RINGS, k].astype(F32)
        c0[k] = total
    c0c = remote(c0.at[1 - h], rc, hs.at[2], hr.at[2], across)

    take_forward(5)
    finish_grad(5)
    s3c.wait_recv()
    scale_grad = jnp.sum(s3[...] + s3r[...], axis=0, keepdims=True)
    factor = -scale_grad * mag[...] / (norm * norm * norm)
    mg[...] = scale_grad / norm / REPLICAS
    columns = jnp.concatenate([scale, factor, jnp.zeros((6, COLS), F32)], axis=0)
    cv[...] = columns.T
    o4c.wait_recv()
    mine = pl.ds(pl.multiple_of(d * OUTROWS, OUTROWS), OUTROWS)
    direct = o4[h][:, :RANK] + o4r[:, pl.ds(0, RANK)]
    shared = o2[c, z * 2 + h][:, RANK:]
    og[...] = (direct * cv[mine, pl.ds(0, 1)] + shared * cv[mine, pl.ds(1, 1)]) / REPLICAS
    turned = a[...].astype(F32) * factor
    thi, tlo = halves(turned)
    part = pl.ds(pl.multiple_of(d * SHARE, SHARE), SHARE)
    wsh = wv[part, :]
    small = mm(thi, a[...], 1, 1) + mm(tlo, a[...], 1, 1)
    term = mm(thi, wsh, 1, 1) + mm(tlo, wsh, 1, 1) + mm2(small, lv[pl.ds(TOK, RANK), part], 1, 0)

    take_forward(6)
    finish_grad(6)
    c0c.wait_recv()
    ig[...] = (c0[h] + rc[...] + term) / REPLICAS
    fpc.wait_recv()

    take_forward(7)
    keys[...] = ((partial_keys() + fpr[...]) * scale).astype(BF)
    finish_grad(7)

    for cp in [kcp, sqc, s0c, oxc, indc, s1c, o2c, fpc, s3c, o4c, c0c] + zsc + o3c + sbc + fwd + grad:
        cp.wait_send()


def hand_over(*results):
    count = len(results)

    def copies(*refs):
        moves = [
            pltpu.make_async_copy(refs[i], refs[count + i], refs[-1].at[i]) for i in range(count)
        ]
        for cp in moves:
            cp.start()
        for cp in moves:
            cp.wait()

    return pl.pallas_call(
        copies,
        out_shape=[jax.ShapeDtypeStruct(r.shape, r.dtype) for r in results],
        in_specs=[pl.BlockSpec(memory_space=pl.ANY)] * count,
        out_specs=[pl.BlockSpec(memory_space=pl.ANY)] * count,
        scratch_shapes=[pltpu.SemaphoreType.DMA((count,))],
        compiler_params=pltpu.CompilerParams(vmem_limit_bytes=2**20),
        name="hand_over",
    )(*results)


def per_device(section_out, saved_stream, section_grad, key_grad, key_weight, adapter_in, adapter_out, magnitude):
    vmem = pl.BlockSpec(memory_space=pltpu.VMEM)
    hbm = pl.BlockSpec(memory_space=pl.ANY)
    dma = pltpu.SemaphoreType.DMA
    V = pltpu.VMEM
    half = REPLICAS // 2
    keys, so, mg, og, ig = pl.pallas_call(
        kernel,
        out_shape=[
            V((HALF, COLS), BF),
            V((TOK, FEAT), BF),
            V((1, COLS), F32),
            V((OUTROWS, RANK), F32),
            V((RANK, SHARE), F32),
        ],
        in_specs=[hbm] * 8,
        out_specs=[vmem] * 5,
        scratch_shapes=[
            V((RANK, COLS), BF),
            V((1, COLS), F32),
            V((FEAT, COLS), BF),
            V((TOK + RANK, FEAT), BF),
            V((TOK, FEAT), BF),
            V((TOK, FEAT), BF),
            V((TOK, FEAT), F32),
            V((2, HALF, COLS), BF),
            V((TOK + RANK, COLS), F32),
            V((TOK + RANK, RANK), F32),
            V((8, COLS), F32),
            V((8, COLS), F32),
            V((TOK, COLS), BF),
            V((TOK, RANK), BF),
            V((HALF, COLS), F32),
            V((HALF, RANK), F32),
            V((COLS, 2 * RANK), F32),
            V((COLS, 2 * RANK), F32),
            V((2, half, OUTROWS, 2 * RANK), F32),
            V((half, OUTROWS, 2 * RANK), F32),
            V((RINGS, 2, OUTROWS, 2 * RANK), F32),
            V((RINGS, 2, OUTROWS, 2 * RANK), F32),
            V((2, OUTROWS, 2 * RANK), F32),
            V((OUTROWS, 2 * RANK), F32),
            V((8, COLS), F32),
            V((8, COLS), F32),
            V((8, COLS), F32),
            V((8, COLS), F32),
            V((RINGS, 8, COLS), F32),
            V((8, COLS), F32),
            V((8, COLS), F32),
            V((2, half, RANK, SHARE), F32),
            V((half, RANK, SHARE), F32),
            V((RINGS, 2, RANK, SHARE), BF),
            V((RINGS, 2, RANK, SHARE), BF),
            V((2, RANK, SHARE), F32),
            V((RANK, SHARE), F32),
            V((HALF, COLS), F32),
            V((HALF, COLS), F32),
            V((COLS, 8), F32),
            dma((9,)),
            dma((GRAD_PIECES,)),
            dma((GRAD_PIECES,)),
            dma((GRAD_PIECES,)),
            dma((GRAD_PIECES,)),
            dma((5,)),
            dma((5,)),
            dma((3,)),
            dma((3,)),
            dma((21,)),
            dma((21,)),
            dma((3,)),
            dma((3,)),
            pltpu.SemaphoreType.REGULAR((3,)),
        ],
        compiler_params=pltpu.CompilerParams(
            collective_id=0, has_side_effects=True, vmem_limit_bytes=40 * 2**20
        ),
        name="relay_tick",
    )(
        *[
            pltpu.with_memory_space_constraint(value, pltpu.HBM)
            for value in (
                section_out[0], saved_stream[0], section_grad[0], key_grad[0],
                key_weight[0], adapter_in[0].T, adapter_out[0], magnitude,
            )
        ]
    )
    keys, so, mg, og, ig = hand_over(keys, so, mg, og, ig)
    return (keys[None], so[None], mg, og.T[None], ig.T[None])


def solution(mesh):
    placed = (
        P("pipe", "dp", "tensor"),
        P("pipe", "dp", "tensor"),
        P("pipe", "dp", "tensor"),
        P("pipe", ("dp", "tensor"), None),
        P("pipe", "tensor", None),
        P("pipe", "tensor", None),
        P("pipe", None, None),
        P("pipe", None),
    )
    return jax.shard_map(
        per_device,
        mesh=mesh,
        in_specs=placed,
        out_specs=(
            P("pipe", ("dp", "tensor"), None),
            P("pipe", "dp", "tensor"),
            P("pipe", None),
            P("pipe", None, "dp"),
            P("pipe", ("tensor", "dp"), None),
        ),
        check_vma=False,
    )
```

```python
import jax
import jax.numpy as jnp
from jax import lax
from jax.experimental import pallas as pl
from jax.experimental.pallas import tpu as pltpu
from jax.sharding import PartitionSpec as P

EPSILON = 1e-06
MESH = pl.DeviceIdType.MESH
BF = jnp.bfloat16
F32 = jnp.float32

PIPES = 4
REPLICAS = 32
HUB = 2
RINGS = 8
TOK = 128
HALF = 64
COLS = 512
RANK = 64
FEAT = 8192
SHARE = FEAT // REPLICAS
OUTROWS = COLS // REPLICAS
DEPTH = 512
STREAM = 1024
FWD_PIECES = (
    (False, 0, 4096),
    (False, 4096, 4096),
    (True, 0, 4096),
    (True, 4096, 2048),
    (True, 6144, 1536),
    (True, 7680, 512),
)
GRAD_PIECES = 8
GRAD_ROWS = TOK // GRAD_PIECES


def mm(left, right, left_dim, right_dim):
    return lax.dot_general(
        left, right, (((left_dim,), (right_dim,)), ((), ())), preferred_element_type=F32
    )


def halves(value):
    upper = value.astype(BF)
    lower = (value - upper.astype(F32)).astype(BF)
    return upper, lower


def mm2(wide, narrow, left_dim, right_dim):
    upper, lower = halves(wide)
    return mm(upper, narrow, left_dim, right_dim) + mm(lower, narrow, left_dim, right_dim)


def kernel(
    x, sv, sg, kg, w, bt, a_in, mag_in,
    keys, so, mg, og, ig,
    a, mag, wv, bv, lv, fw, gr, sp, kc, raw, low, sqs, ksb, lgv, fac, flo,
    ox, oxr, o2, o2r, o3, o3r, o4, o4r,
    s0, s0r, s1, s1r, zs, s3, s3r,
    im, io, ra, sb, rb, c0, rc, fp, fpr, cv,
    loc, fs, fr, gs, gf, ts, tr, cs, cr, zsd, zrv, hs, hr, qs, qr, know,
):
    p = lax.axis_index("pipe")
    d = lax.axis_index("dp")
    t = lax.axis_index("tensor")
    z, h, c = d // 4, (d // 2) % 2, d % 2

    def dev(p_=p, z_=z, h_=h, c_=c, t_=t):
        return {"pipe": p_, "dp": (z_ * 2 + h_) * 2 + c_, "tensor": t_}

    up, down = dev(p_=(p + 1) % PIPES), dev(p_=(p + PIPES - 1) % PIPES)
    pair, mate, across = dev(t_=1 - t), dev(c_=1 - c), dev(h_=1 - h)
    both_other = dev(t_=1 - t, c_=1 - c)
    ring = [dev(z_=(z + k) % RINGS) for k in range(1, RINGS)]

    def remote(src, dst, ssem, rsem, to):
        cp = pltpu.make_async_remote_copy(
            src_ref=src, dst_ref=dst, send_sem=ssem, recv_sem=rsem, device_id=to, device_id_type=MESH
        )
        cp.start()
        return cp

    mine = pl.ds(pl.multiple_of(c * (FEAT // 2), FEAT // 2), FEAT // 2)
    others = pl.ds(pl.multiple_of((1 - c) * (FEAT // 2), FEAT // 2), FEAT // 2)
    first = [
        pltpu.make_async_copy(a_in, a, loc.at[0]),
        pltpu.make_async_copy(mag_in, mag, loc.at[1]),
        pltpu.make_async_copy(bt, bv, loc.at[2]),
        pltpu.make_async_copy(w.at[mine], wv.at[mine], loc.at[3]),
    ]
    second = [
        pltpu.make_async_copy(kg, kc.at[t], loc.at[4]),
        pltpu.make_async_copy(sv, lv, loc.at[5]),
        pltpu.make_async_copy(w.at[others], wv.at[others], loc.at[6]),
    ]
    for cp in first + second:
        cp.start()

    def signal(sem, to):
        pl.semaphore_signal(sem, inc=1, device_id=to, device_id_type=MESH)

    def meet(sem, step):
        @pl.when(z >= step)
        def _():
            signal(sem, dev(z_=z - step))

        @pl.when(z + step < RINGS)
        def _():
            signal(sem, dev(z_=z + step))

    def met(step):
        return jnp.where(z >= step, 1, 0) + jnp.where(z + step < RINGS, 1, 0)

    barrier = pltpu.get_barrier_semaphore()
    near = [up, down, pair, mate, both_other]
    for to in near:
        signal(barrier, to)

    @pl.when(p == HUB)
    def _():
        signal(barrier, across)
        meet(barrier, 1)

    pl.semaphore_wait(barrier, len(near) + jnp.where(p == HUB, 1 + met(1), 0))

    fwd, grad = [], []
    for i in range(len(FWD_PIECES)):
        own, start, width = FWD_PIECES[i]
        rows = pl.ds(pl.multiple_of((t if own else 1 - t) * HALF, HALF), HALF)
        at = (rows, pl.ds(start, width))
        fwd.append(remote(x.at[at], fw.at[at], fs.at[i], fr.at[i], up))
    for i in range(GRAD_PIECES):
        at = pl.ds(i * GRAD_ROWS, GRAD_ROWS)
        grad.append(remote(sg.at[at], gr.at[at], gs.at[i], gf.at[i], down))
    kcp = remote(kg, kc.at[t], ts.at[0], tr.at[0], pair)

    @pl.when(p == HUB - 1)
    def _():
        signal(know.at[0], up)

    @pl.when(p == HUB)
    def _():
        pl.semaphore_wait(know.at[0], 1)
        signal(know.at[1], across)
        meet(know.at[1], 1)

    here = t * 2 + c
    sqs[here] = jnp.zeros((8, COLS), F32)
    for cp in first:
        cp.wait()
    av = a[...]

    @pl.when(p == HUB)
    def _():
        pl.semaphore_wait(know.at[1], 1 + met(1))
        meet(know.at[2], 2)

    @pl.loop(0, FEAT // 2 // DEPTH)
    def _(i):
        part = pl.ds(pl.multiple_of(c * (FEAT // 2) + i * DEPTH, DEPTH), DEPTH)
        combined = wv[part, :].astype(F32) + mm(bv[:, part], a[...], 0, 0)
        sqs[here] += jnp.sum((combined * combined).reshape(DEPTH // 8, 8, COLS), axis=0)

    sqc = [
        remote(sqs.at[here], sqs.at[here], qs.at[k], qr.at[k], to)
        for k, to in enumerate([pair, mate, both_other])
    ]

    @pl.when(p == HUB)
    def _():
        pl.semaphore_wait(know.at[2], met(2))
        meet(know.at[3], 4)

    raw[...] = jnp.zeros_like(raw)
    low[...] = jnp.zeros_like(low)
    for cp in second:
        cp.wait()

    @pl.loop(0, FEAT // DEPTH)
    def _(i):
        part = pl.ds(pl.multiple_of(i * DEPTH, DEPTH), DEPTH)
        left = lv[:, part]
        raw[...] += mm(left, wv[part, :], 1, 0)
        low[...] += mm(left, bv[:, part], 1, 1)

    kcp.wait_recv()
    cot = kc[...].reshape(TOK, COLS)
    for cp in sqc:
        cp.wait_recv()
    norm = jnp.sqrt(
        jnp.sum((sqs[0] + sqs[1]) + (sqs[2] + sqs[3]), axis=0, keepdims=True) + EPSILON
    )
    scale = mag[...] / norm
    shi, slo = halves(cot.astype(F32) * scale)
    ksb[...] = shi
    low_grad = mm(shi, av, 1, 1) + mm(slo, av, 1, 1)
    lgv[...] = low_grad.astype(BF)
    turned_grad = low_grad.T.astype(BF)

    def token_sum(i, core):
        part = pl.ds(pl.multiple_of((i * 2 + core) * SHARE, SHARE), SHARE)
        return mm(turned_grad, lv[:, part], 1, 0)

    @pl.loop(0, REPLICAS // 2)
    def _(i):
        im[i] = token_sum(i, 1 - c)

    imc = remote(im, ra, cs.at[0], cr.at[0], mate)

    @pl.when(p == HUB)
    def _():
        pl.semaphore_wait(know.at[3], met(4))
        signal(know.at[4], up)
        signal(know.at[4], down)

    lhi, llo = halves(low[...])
    raw_saved = raw[...] + mm(lhi, av, 1, 0) + mm(llo, av, 1, 0)
    s0[...] = jnp.sum((cot.astype(F32) * raw_saved).reshape(TOK // 8, 8, COLS), axis=0)
    s0c = remote(s0, s0r, ts.at[1], tr.at[1], pair)
    part = pl.ds(pl.multiple_of(d * SHARE, SHARE), SHARE)
    b_share = bv[:, part]
    cross = mm(b_share, wv[part, :], 1, 0) + mm2(mm(b_share, b_share, 1, 1), av, 1, 0)
    ox[:, pl.ds(0, RANK)] = mm(cot, lhi, 0, 0) + mm(cot, llo, 0, 0)
    ox[:, pl.ds(RANK, RANK)] = cross.T
    oxc = remote(ox, oxr, ts.at[2], tr.at[2], pair)

    @pl.when(p == HUB - 1)
    def _():
        pl.semaphore_wait(know.at[4], 1)
        signal(know.at[4], down)

    @pl.loop(0, REPLICAS // 2)
    def _(i):
        io[i] = token_sum(i, c)

    s0c.wait_recv()
    s1[...] = s0[...] + s0r[...]
    s1c = remote(s1, s1r, cs.at[1], cr.at[1], mate)

    imc.wait_recv()

    @pl.when((p == HUB + 1) | (p == HUB - 2))
    def _():
        pl.semaphore_wait(know.at[4], 1)

    @pl.loop(0, RINGS)
    def _(i):
        for k in range(2):
            sb[i, k] = (io[i * 2 + k] + ra[i * 2 + k]).astype(BF)

    sbc = [
        remote(sb.at[(z + k + 1) % RINGS], rb.at[z], zsd.at[14 + k], zrv.at[14 + k], to)
        for k, to in enumerate(ring)
    ]

    oxc.wait_recv()
    sums = (ox[...] + oxr[...]).reshape(REPLICAS // 2, 2, OUTROWS, 2 * RANK)
    o2[0] = sums[:, 0]
    o2[1] = sums[:, 1]
    o2c = remote(o2.at[1 - c], o2r, cs.at[2], cr.at[2], mate)

    def stream_piece(i):
        part = pl.ds(pl.multiple_of(i * STREAM, STREAM), STREAM)
        sp[:, part] = mm(ksb[...], wv[part, :], 1, 1) + mm(lgv[...], bv[:, part], 1, 0)

    pl.loop(0, FEAT // STREAM // 2)(stream_piece)

    s1c.wait_recv()
    zs[z] = s1[...] + s1r[...]
    zsc = [remote(zs.at[z], zs.at[z], zsd.at[k], zrv.at[k], to) for k, to in enumerate(ring)]
    o2c.wait_recv()
    o3[...] = (o2[c] + o2r[...]).reshape(RINGS, 2, OUTROWS, 2 * RANK)
    o3c = [
        remote(o3.at[(z + k + 1) % RINGS], o3r.at[z], zsd.at[7 + k], zrv.at[7 + k], to)
        for k, to in enumerate(ring)
    ]

    pl.loop(FEAT // STREAM // 2, FEAT // STREAM)(stream_piece)

    def finish_grad(i):
        grad[i].wait_recv()
        at = pl.ds(i * GRAD_ROWS, GRAD_ROWS)
        so[at] = (sp[at] + gr[at].astype(F32)).astype(BF)

    def take_forward(i):
        fwd[i].wait_recv()
        own, start, width = FWD_PIECES[i]
        rows = pl.ds(pl.multiple_of((t if own else 1 - t) * HALF, HALF), HALF)
        if start == 0:
            fac[...] = jnp.zeros_like(fac)
            flo[...] = jnp.zeros_like(flo)

        @pl.loop(0, width // DEPTH)
        def _(k):
            part = pl.ds(pl.multiple_of(start + k * DEPTH, DEPTH), DEPTH)
            rowsv = fw[rows, part]
            fac[...] += mm(rowsv, wv[part, :], 1, 0)
            flo[...] += mm(rowsv, bv[:, part], 1, 1)

    def partial_keys():
        return fac[...] + mm2(flo[...], a[...], 1, 0)

    take_forward(0)
    finish_grad(0)
    take_forward(1)
    finish_grad(1)
    finish_grad(2)
    finish_grad(3)
    fp[...] = partial_keys()
    fpc = remote(fp, fpr, ts.at[3], tr.at[3], pair)

    for cp in zsc:
        cp.wait_recv()
    total = zs[0]
    for k in range(1, RINGS):
        total = total + zs[k]
    s3[...] = total
    s3c = remote(s3, s3r, hs.at[0], hr.at[0], across)
    for cp in o3c:
        cp.wait_recv()
    total = o3[z]
    for k in range(1, RINGS):
        total = total + o3r[(z + k) % RINGS]
    o4[...] = total
    o4c = remote(o4.at[1 - h], o4r, hs.at[1], hr.at[1], across)

    for cp in sbc:
        cp.wait_recv()
    for k in range(2):
        total = io[z * 2 + k] + ra[z * 2 + k]
        for n in range(1, RINGS):
            total = total + rb[(z + n) % RINGS, k].astype(F32)
        c0[k] = total
    c0c = remote(c0.at[1 - h], rc, hs.at[2], hr.at[2], across)

    take_forward(2)
    finish_grad(4)
    s3c.wait_recv()
    scale_grad = jnp.sum(s3[...] + s3r[...], axis=0, keepdims=True)
    factor = -scale_grad * mag[...] / (norm * norm * norm)
    mg[...] = scale_grad / norm / REPLICAS
    columns = jnp.concatenate([scale, factor, jnp.zeros((6, COLS), F32)], axis=0)
    cv[...] = columns.T
    o4c.wait_recv()
    lines = pl.ds(pl.multiple_of(d * OUTROWS, OUTROWS), OUTROWS)
    whole = o4[h] + o4r[...]
    og[...] = (
        whole[:, :RANK] * cv[lines, pl.ds(0, 1)] + whole[:, RANK:] * cv[lines, pl.ds(1, 1)]
    ) / REPLICAS
    turned = a[...].astype(F32) * factor
    thi, tlo = halves(turned)
    part = pl.ds(pl.multiple_of(d * SHARE, SHARE), SHARE)
    wsh = wv[part, :]
    small = mm(thi, a[...], 1, 1) + mm(tlo, a[...], 1, 1)
    term = mm(thi, wsh, 1, 1) + mm(tlo, wsh, 1, 1) + mm2(small, bv[:, part], 1, 0)

    finish_grad(5)
    take_forward(3)
    c0c.wait_recv()
    ig[...] = (c0[h] + rc[...] + term) / REPLICAS
    fpc.wait_recv()
    finish_grad(6)
    take_forward(4)
    take_forward(5)
    keys[...] = ((partial_keys() + fpr[...]) * scale).astype(BF)
    finish_grad(7)

    for cp in [kcp, s0c, oxc, imc, s1c, o2c, fpc, s3c, o4c, c0c] + sqc + zsc + o3c + sbc + fwd + grad:
        cp.wait_send()


def hand_over(*results):
    count = len(results)
    places = []
    for i, value in enumerate(results):
        rows = value.shape[0]
        cuts = 8 if rows == TOK else 1
        places += [(i, pl.ds(k * (rows // cuts), rows // cuts)) for k in range(cuts)]

    def copies(*refs):
        moves = [
            pltpu.make_async_copy(refs[i].at[at], refs[count + i].at[at], refs[-1].at[k])
            for k, (i, at) in enumerate(places)
        ]
        for cp in moves:
            cp.start()
        for cp in moves:
            cp.wait()

    return pl.pallas_call(
        copies,
        out_shape=[jax.ShapeDtypeStruct(r.shape, r.dtype) for r in results],
        in_specs=[pl.BlockSpec(memory_space=pl.ANY)] * count,
        out_specs=[pl.BlockSpec(memory_space=pl.ANY)] * count,
        scratch_shapes=[pltpu.SemaphoreType.DMA((len(places),))],
        compiler_params=pltpu.CompilerParams(vmem_limit_bytes=2**20),
        name="hand_over",
    )(*results)


def per_device(section_out, saved_stream, section_grad, key_grad, key_weight, adapter_in, adapter_out, magnitude):
    vmem = pl.BlockSpec(memory_space=pltpu.VMEM)
    hbm = pl.BlockSpec(memory_space=pl.ANY)
    dma = pltpu.SemaphoreType.DMA
    V = pltpu.VMEM
    half = REPLICAS // 2
    keys, so, mg, og, ig = pl.pallas_call(
        kernel,
        out_shape=[
            V((HALF, COLS), BF),
            V((TOK, FEAT), BF),
            V((1, COLS), F32),
            V((OUTROWS, RANK), F32),
            V((RANK, SHARE), F32),
        ],
        in_specs=[hbm] * 8,
        out_specs=[vmem] * 5,
        scratch_shapes=[
            V((RANK, COLS), BF),
            V((1, COLS), F32),
            V((FEAT, COLS), BF),
            V((RANK, FEAT), BF),
            V((TOK, FEAT), BF),
            V((TOK, FEAT), BF),
            V((TOK, FEAT), BF),
            V((TOK, FEAT), F32),
            V((2, HALF, COLS), BF),
            V((TOK, COLS), F32),
            V((TOK, RANK), F32),
            V((4, 8, COLS), F32),
            V((TOK, COLS), BF),
            V((TOK, RANK), BF),
            V((HALF, COLS), F32),
            V((HALF, RANK), F32),
            V((COLS, 2 * RANK), F32),
            V((COLS, 2 * RANK), F32),
            V((2, half, OUTROWS, 2 * RANK), F32),
            V((half, OUTROWS, 2 * RANK), F32),
            V((RINGS, 2, OUTROWS, 2 * RANK), F32),
            V((RINGS, 2, OUTROWS, 2 * RANK), F32),
            V((2, OUTROWS, 2 * RANK), F32),
            V((OUTROWS, 2 * RANK), F32),
            V((8, COLS), F32),
            V((8, COLS), F32),
            V((8, COLS), F32),
            V((8, COLS), F32),
            V((RINGS, 8, COLS), F32),
            V((8, COLS), F32),
            V((8, COLS), F32),
            V((half, RANK, SHARE), F32),
            V((half, RANK, SHARE), F32),
            V((half, RANK, SHARE), F32),
            V((RINGS, 2, RANK, SHARE), BF),
            V((RINGS, 2, RANK, SHARE), BF),
            V((2, RANK, SHARE), F32),
            V((RANK, SHARE), F32),
            V((HALF, COLS), F32),
            V((HALF, COLS), F32),
            V((COLS, 8), F32),
            dma((7,)),
            dma((len(FWD_PIECES),)),
            dma((len(FWD_PIECES),)),
            dma((GRAD_PIECES,)),
            dma((GRAD_PIECES,)),
            dma((4,)),
            dma((4,)),
            dma((3,)),
            dma((3,)),
            dma((21,)),
            dma((21,)),
            dma((3,)),
            dma((3,)),
            dma((3,)),
            dma((3,)),
            pltpu.SemaphoreType.REGULAR((5,)),
        ],
        compiler_params=pltpu.CompilerParams(
            collective_id=0, has_side_effects=True, vmem_limit_bytes=40 * 2**20
        ),
        name="relay_tick",
    )(
        *[
            pltpu.with_memory_space_constraint(value, pltpu.HBM)
            for value in (
                section_out[0], saved_stream[0], section_grad[0], key_grad[0],
                key_weight[0], adapter_in[0].T, adapter_out[0], magnitude,
            )
        ]
    )
    keys, so, mg, og, ig = hand_over(keys, so, mg, og, ig)
    return (keys[None], so[None], mg, og.T[None], ig.T[None])


def solution(mesh):
    placed = (
        P("pipe", "dp", "tensor"),
        P("pipe", "dp", "tensor"),
        P("pipe", "dp", "tensor"),
        P("pipe", ("dp", "tensor"), None),
        P("pipe", "tensor", None),
        P("pipe", "tensor", None),
        P("pipe", None, None),
        P("pipe", None),
    )
    return jax.shard_map(
        per_device,
        mesh=mesh,
        in_specs=placed,
        out_specs=(
            P("pipe", ("dp", "tensor"), None),
            P("pipe", "dp", "tensor"),
            P("pipe", None),
            P("pipe", None, "dp"),
            P("pipe", ("tensor", "dp"), None),
        ),
        check_vma=False,
    )
```

```python
import jax
import jax.numpy as jnp
from jax import lax
from jax.experimental import pallas as pl
from jax.experimental.pallas import tpu as pltpu
from jax.sharding import PartitionSpec as P

EPSILON = 1e-06
MESH = pl.DeviceIdType.MESH
BF = jnp.bfloat16
F32 = jnp.float32

PIPES = 4
REPLICAS = 32
HUB = 2
RINGS = 8
TOK = 128
HALF = 64
COLS = 512
RANK = 64
FEAT = 8192
SHARE = FEAT // REPLICAS
OUTROWS = COLS // REPLICAS
DEPTH = 512
STREAM = 1024
FWD_PIECES = (
    (False, 0, 4096),
    (False, 4096, 4096),
    (True, 0, 4096),
    (True, 4096, 2048),
    (True, 6144, 1536),
    (True, 7680, 512),
)
GRAD_PIECES = 8
GRAD_ROWS = TOK // GRAD_PIECES


def mm(left, right, left_dim, right_dim):
    return lax.dot_general(
        left, right, (((left_dim,), (right_dim,)), ((), ())), preferred_element_type=F32
    )


def halves(value):
    upper = value.astype(BF)
    lower = (value - upper.astype(F32)).astype(BF)
    return upper, lower


def mm2(wide, narrow, left_dim, right_dim):
    upper, lower = halves(wide)
    return mm(upper, narrow, left_dim, right_dim) + mm(lower, narrow, left_dim, right_dim)


def kernel(
    x, sv, sg, kg, w, bt, a_in, mag_in,
    keys, so, mg, og, ig,
    a, mag, wv, bv, lv, fw, gr, sp, kc, raw, low, sqs, ksb, lgv, fac, flo,
    ox, oxr, o2, o2r, o3, o3r, o4, o4r,
    s0, s0r, s1, s1r, zs, s3, s3r,
    im, io, ra, sb, rb, c0, rc, fp, fpr, cv,
    loc, fs, fr, gs, gf, ts, tr, cs, cr, zsd, zrv, hs, hr, qs, qr, know,
):
    p = lax.axis_index("pipe")
    d = lax.axis_index("dp")
    t = lax.axis_index("tensor")
    z, h, c = d // 4, (d // 2) % 2, d % 2

    def dev(p_=p, z_=z, h_=h, c_=c, t_=t):
        return {"pipe": p_, "dp": (z_ * 2 + h_) * 2 + c_, "tensor": t_}

    up, down = dev(p_=(p + 1) % PIPES), dev(p_=(p + PIPES - 1) % PIPES)
    pair, mate, across = dev(t_=1 - t), dev(c_=1 - c), dev(h_=1 - h)
    both_other = dev(t_=1 - t, c_=1 - c)
    ring = [dev(z_=(z + k) % RINGS) for k in range(1, RINGS)]

    def remote(src, dst, ssem, rsem, to):
        cp = pltpu.make_async_remote_copy(
            src_ref=src, dst_ref=dst, send_sem=ssem, recv_sem=rsem, device_id=to, device_id_type=MESH
        )
        cp.start()
        return cp

    def signal(sem, to):
        pl.semaphore_signal(sem, inc=1, device_id=to, device_id_type=MESH)

    def meet(sem, step):
        @pl.when(z >= step)
        def _():
            signal(sem, dev(z_=z - step))

        @pl.when(z + step < RINGS)
        def _():
            signal(sem, dev(z_=z + step))

    def met(step):
        return jnp.where(z >= step, 1, 0) + jnp.where(z + step < RINGS, 1, 0)

    barrier = pltpu.get_barrier_semaphore()
    near = [up, down, mate]
    hub, hub_mate = (p == HUB) & (c == 0), (p == HUB) & (c == 1)
    below, ends = p == HUB - 1, (p == HUB + 1) | (p == HUB - 2)
    for to in near:
        signal(barrier, to)

    @pl.when(hub)
    def _():
        signal(barrier, pair)
        signal(barrier, across)
        meet(barrier, 1)

    mine = pl.ds(pl.multiple_of(c * (FEAT // 2), FEAT // 2), FEAT // 2)
    others = pl.ds(pl.multiple_of((1 - c) * (FEAT // 2), FEAT // 2), FEAT // 2)
    first = [
        pltpu.make_async_copy(a_in, a, loc.at[0]),
        pltpu.make_async_copy(mag_in, mag, loc.at[1]),
        pltpu.make_async_copy(bt, bv, loc.at[2]),
        pltpu.make_async_copy(w.at[mine], wv.at[mine], loc.at[3]),
    ]
    second = [
        pltpu.make_async_copy(kg, kc.at[t], loc.at[4]),
        pltpu.make_async_copy(sv, lv, loc.at[5]),
        pltpu.make_async_copy(w.at[others], wv.at[others], loc.at[6]),
    ]
    for cp in first + second:
        cp.start()

    pl.semaphore_wait(barrier, len(near) + jnp.where(hub, 2 + met(1), 0))

    fwd, grad = [], []
    for i in range(GRAD_PIECES):
        if i < len(FWD_PIECES):
            own, start, width = FWD_PIECES[i]
            rows = pl.ds(pl.multiple_of((t if own else 1 - t) * HALF, HALF), HALF)
            at = (rows, pl.ds(start, width))
            fwd.append(remote(x.at[at], fw.at[at], fs.at[i], fr.at[i], up))
        at = pl.ds(i * GRAD_ROWS, GRAD_ROWS)
        grad.append(remote(sg.at[at], gr.at[at], gs.at[i], gf.at[i], down))

    @pl.when(below)
    def _():
        signal(know.at[0], up)

    @pl.when(hub_mate)
    def _():
        pl.semaphore_wait(know.at[0], 1)
        signal(know.at[0], mate)

    @pl.when(hub)
    def _():
        pl.semaphore_wait(know.at[0], 2)
        signal(know.at[5], pair)
        signal(know.at[1], across)
        meet(know.at[1], 1)
        pl.semaphore_wait(know.at[5], 1)
        for to in near:
            signal(know.at[6], to)

    here = t * 2 + c
    sqs[here] = jnp.zeros((8, COLS), F32)
    for cp in first:
        cp.wait()
    av = a[...]

    @pl.when(hub_mate)
    def _():
        pl.semaphore_wait(know.at[6], 1)
        signal(know.at[6], up)
        signal(know.at[6], down)

    @pl.when(hub)
    def _():
        pl.semaphore_wait(know.at[1], 1 + met(1))
        meet(know.at[2], 2)

    @pl.loop(0, FEAT // 2 // DEPTH)
    def _(i):
        part = pl.ds(pl.multiple_of(c * (FEAT // 2) + i * DEPTH, DEPTH), DEPTH)
        combined = wv[part, :].astype(F32) + mm(bv[:, part], a[...], 0, 0)
        sqs[here] += jnp.sum((combined * combined).reshape(DEPTH // 8, 8, COLS), axis=0)

    @pl.when(below)
    def _():
        pl.semaphore_wait(know.at[6], 1)
        signal(know.at[6], down)

    @pl.when(hub)
    def _():
        pl.semaphore_wait(know.at[2], met(2))
        meet(know.at[3], 4)

    raw[...] = jnp.zeros_like(raw)
    low[...] = jnp.zeros_like(low)
    for cp in second:
        cp.wait()

    def saved_piece(i):
        part = pl.ds(pl.multiple_of(i * DEPTH, DEPTH), DEPTH)
        left = lv[:, part]
        raw[...] += mm(left, wv[part, :], 1, 0)
        low[...] += mm(left, bv[:, part], 1, 1)

    pl.loop(0, FEAT // DEPTH // 2)(saved_piece)

    @pl.when(ends)
    def _():
        pl.semaphore_wait(know.at[6], 1)

    kcp = remote(kg, kc.at[t], ts.at[0], tr.at[0], pair)
    sqc = [
        remote(sqs.at[here], sqs.at[here], qs.at[k], qr.at[k], to)
        for k, to in enumerate([pair, mate, both_other])
    ]

    pl.loop(FEAT // DEPTH // 2, FEAT // DEPTH)(saved_piece)

    kcp.wait_recv()
    cot = kc[...].reshape(TOK, COLS)
    for cp in sqc:
        cp.wait_recv()
    norm = jnp.sqrt(
        jnp.sum((sqs[0] + sqs[1]) + (sqs[2] + sqs[3]), axis=0, keepdims=True) + EPSILON
    )
    scale = mag[...] / norm
    shi, slo = halves(cot.astype(F32) * scale)
    ksb[...] = shi
    low_grad = mm(shi, av, 1, 1) + mm(slo, av, 1, 1)
    lgv[...] = low_grad.astype(BF)
    turned_grad = low_grad.T.astype(BF)

    def token_sum(i, core):
        part = pl.ds(pl.multiple_of((i * 2 + core) * SHARE, SHARE), SHARE)
        return mm(turned_grad, lv[:, part], 1, 0)

    @pl.loop(0, REPLICAS // 2)
    def _(i):
        im[i] = token_sum(i, 1 - c)

    imc = remote(im, ra, cs.at[0], cr.at[0], mate)

    @pl.when(hub)
    def _():
        pl.semaphore_wait(know.at[3], met(4))
        for to in near:
            signal(know.at[4], to)

    lhi, llo = halves(low[...])
    raw_saved = raw[...] + mm(lhi, av, 1, 0) + mm(llo, av, 1, 0)
    s0[...] = jnp.sum((cot.astype(F32) * raw_saved).reshape(TOK // 8, 8, COLS), axis=0)
    s0c = remote(s0, s0r, ts.at[1], tr.at[1], pair)
    part = pl.ds(pl.multiple_of(d * SHARE, SHARE), SHARE)
    b_share = bv[:, part]
    cross = mm(b_share, wv[part, :], 1, 0) + mm2(mm(b_share, b_share, 1, 1), av, 1, 0)
    ox[:, pl.ds(0, RANK)] = mm(cot, lhi, 0, 0) + mm(cot, llo, 0, 0)
    ox[:, pl.ds(RANK, RANK)] = cross.T
    oxc = remote(ox, oxr, ts.at[2], tr.at[2], pair)

    @pl.when(hub_mate)
    def _():
        pl.semaphore_wait(know.at[4], 1)
        signal(know.at[4], up)
        signal(know.at[4], down)

    @pl.loop(0, REPLICAS // 2)
    def _(i):
        io[i] = token_sum(i, c)

    @pl.when(below)
    def _():
        pl.semaphore_wait(know.at[4], 1)
        signal(know.at[4], down)

    s0c.wait_recv()
    s1[...] = s0[...] + s0r[...]
    s1c = remote(s1, s1r, cs.at[1], cr.at[1], mate)

    imc.wait_recv()

    @pl.when(ends)
    def _():
        pl.semaphore_wait(know.at[4], 1)

    @pl.loop(0, RINGS)
    def _(i):
        for k in range(2):
            sb[i, k] = (io[i * 2 + k] + ra[i * 2 + k]).astype(BF)

    sbc = [
        remote(sb.at[(z + k + 1) % RINGS], rb.at[z], zsd.at[14 + k], zrv.at[14 + k], to)
        for k, to in enumerate(ring)
    ]

    oxc.wait_recv()
    sums = (ox[...] + oxr[...]).reshape(REPLICAS // 2, 2, OUTROWS, 2 * RANK)
    o2[0] = sums[:, 0]
    o2[1] = sums[:, 1]
    o2c = remote(o2.at[1 - c], o2r, cs.at[2], cr.at[2], mate)

    def stream_piece(i):
        part = pl.ds(pl.multiple_of(i * STREAM, STREAM), STREAM)
        sp[:, part] = mm(ksb[...], wv[part, :], 1, 1) + mm(lgv[...], bv[:, part], 1, 0)

    pl.loop(0, FEAT // STREAM // 2)(stream_piece)

    s1c.wait_recv()
    zs[z] = s1[...] + s1r[...]
    zsc = [remote(zs.at[z], zs.at[z], zsd.at[k], zrv.at[k], to) for k, to in enumerate(ring)]
    o2c.wait_recv()
    o3[...] = (o2[c] + o2r[...]).reshape(RINGS, 2, OUTROWS, 2 * RANK)
    o3c = [
        remote(o3.at[(z + k + 1) % RINGS], o3r.at[z], zsd.at[7 + k], zrv.at[7 + k], to)
        for k, to in enumerate(ring)
    ]

    pl.loop(FEAT // STREAM // 2, FEAT // STREAM)(stream_piece)

    def finish_grad(i):
        grad[i].wait_recv()
        at = pl.ds(i * GRAD_ROWS, GRAD_ROWS)
        so[at] = (sp[at] + gr[at].astype(F32)).astype(BF)

    def take_forward(i):
        fwd[i].wait_recv()
        own, start, width = FWD_PIECES[i]
        rows = pl.ds(pl.multiple_of((t if own else 1 - t) * HALF, HALF), HALF)
        if start == 0:
            fac[...] = jnp.zeros_like(fac)
            flo[...] = jnp.zeros_like(flo)

        @pl.loop(0, width // DEPTH)
        def _(k):
            part = pl.ds(pl.multiple_of(start + k * DEPTH, DEPTH), DEPTH)
            rowsv = fw[rows, part]
            fac[...] += mm(rowsv, wv[part, :], 1, 0)
            flo[...] += mm(rowsv, bv[:, part], 1, 1)

    def partial_keys():
        return fac[...] + mm2(flo[...], a[...], 1, 0)

    take_forward(0)
    finish_grad(0)
    take_forward(1)
    finish_grad(1)
    finish_grad(2)
    finish_grad(3)
    fp[...] = partial_keys()
    fpc = remote(fp, fpr, ts.at[3], tr.at[3], pair)

    for cp in zsc:
        cp.wait_recv()
    total = zs[0]
    for k in range(1, RINGS):
        total = total + zs[k]
    s3[...] = total
    s3c = remote(s3, s3r, hs.at[0], hr.at[0], across)
    for cp in o3c:
        cp.wait_recv()
    total = o3[z]
    for k in range(1, RINGS):
        total = total + o3r[(z + k) % RINGS]
    o4[...] = total
    o4c = remote(o4.at[1 - h], o4r, hs.at[1], hr.at[1], across)

    for cp in sbc:
        cp.wait_recv()
    for k in range(2):
        total = io[z * 2 + k] + ra[z * 2 + k]
        for n in range(1, RINGS):
            total = total + rb[(z + n) % RINGS, k].astype(F32)
        c0[k] = total
    c0c = remote(c0.at[1 - h], rc, hs.at[2], hr.at[2], across)

    take_forward(2)
    finish_grad(4)
    s3c.wait_recv()
    scale_grad = jnp.sum(s3[...] + s3r[...], axis=0, keepdims=True)
    factor = -scale_grad * mag[...] / (norm * norm * norm)
    mg[...] = scale_grad / norm / REPLICAS
    columns = jnp.concatenate([scale, factor, jnp.zeros((6, COLS), F32)], axis=0)
    cv[...] = columns.T
    o4c.wait_recv()
    lines = pl.ds(pl.multiple_of(d * OUTROWS, OUTROWS), OUTROWS)
    whole = o4[h] + o4r[...]
    og[...] = (
        whole[:, :RANK] * cv[lines, pl.ds(0, 1)] + whole[:, RANK:] * cv[lines, pl.ds(1, 1)]
    ) / REPLICAS
    turned = a[...].astype(F32) * factor
    thi, tlo = halves(turned)
    part = pl.ds(pl.multiple_of(d * SHARE, SHARE), SHARE)
    wsh = wv[part, :]
    small = mm(thi, a[...], 1, 1) + mm(tlo, a[...], 1, 1)
    term = mm(thi, wsh, 1, 1) + mm(tlo, wsh, 1, 1) + mm2(small, bv[:, part], 1, 0)

    finish_grad(5)
    take_forward(3)
    c0c.wait_recv()
    ig[...] = (c0[h] + rc[...] + term) / REPLICAS
    fpc.wait_recv()
    finish_grad(6)
    take_forward(4)
    take_forward(5)
    keys[...] = ((partial_keys() + fpr[...]) * scale).astype(BF)
    finish_grad(7)

    for cp in [kcp, s0c, oxc, imc, s1c, o2c, fpc, s3c, o4c, c0c] + sqc + zsc + o3c + sbc + fwd + grad:
        cp.wait_send()


def hand_over(*results):
    count = len(results)
    places = []
    for i, value in enumerate(results):
        rows = value.shape[0]
        cuts = 2 if rows == TOK else 1
        places += [(i, pl.ds(k * (rows // cuts), rows // cuts)) for k in range(cuts)]

    def copies(*refs):
        moves = [
            pltpu.make_async_copy(refs[i].at[at], refs[count + i].at[at], refs[-1].at[k])
            for k, (i, at) in enumerate(places)
        ]
        for cp in moves:
            cp.start()
        for cp in moves:
            cp.wait()

    return pl.pallas_call(
        copies,
        out_shape=[jax.ShapeDtypeStruct(r.shape, r.dtype) for r in results],
        in_specs=[pl.BlockSpec(memory_space=pl.ANY)] * count,
        out_specs=[pl.BlockSpec(memory_space=pl.ANY)] * count,
        scratch_shapes=[pltpu.SemaphoreType.DMA((len(places),))],
        compiler_params=pltpu.CompilerParams(vmem_limit_bytes=2**20),
        name="hand_over",
    )(*results)


def per_device(section_out, saved_stream, section_grad, key_grad, key_weight, adapter_in, adapter_out, magnitude):
    vmem = pl.BlockSpec(memory_space=pltpu.VMEM)
    hbm = pl.BlockSpec(memory_space=pl.ANY)
    dma = pltpu.SemaphoreType.DMA
    V = pltpu.VMEM
    half = REPLICAS // 2
    keys, so, mg, og, ig = pl.pallas_call(
        kernel,
        out_shape=[
            V((HALF, COLS), BF),
            V((TOK, FEAT), BF),
            V((1, COLS), F32),
            V((OUTROWS, RANK), F32),
            V((RANK, SHARE), F32),
        ],
        in_specs=[hbm] * 8,
        out_specs=[vmem] * 5,
        scratch_shapes=[
            V((RANK, COLS), BF),
            V((1, COLS), F32),
            V((FEAT, COLS), BF),
            V((RANK, FEAT), BF),
            V((TOK, FEAT), BF),
            V((TOK, FEAT), BF),
            V((TOK, FEAT), BF),
            V((TOK, FEAT), F32),
            V((2, HALF, COLS), BF),
            V((TOK, COLS), F32),
            V((TOK, RANK), F32),
            V((4, 8, COLS), F32),
            V((TOK, COLS), BF),
            V((TOK, RANK), BF),
            V((HALF, COLS), F32),
            V((HALF, RANK), F32),
            V((COLS, 2 * RANK), F32),
            V((COLS, 2 * RANK), F32),
            V((2, half, OUTROWS, 2 * RANK), F32),
            V((half, OUTROWS, 2 * RANK), F32),
            V((RINGS, 2, OUTROWS, 2 * RANK), F32),
            V((RINGS, 2, OUTROWS, 2 * RANK), F32),
            V((2, OUTROWS, 2 * RANK), F32),
            V((OUTROWS, 2 * RANK), F32),
            V((8, COLS), F32),
            V((8, COLS), F32),
            V((8, COLS), F32),
            V((8, COLS), F32),
            V((RINGS, 8, COLS), F32),
            V((8, COLS), F32),
            V((8, COLS), F32),
            V((half, RANK, SHARE), F32),
            V((half, RANK, SHARE), F32),
            V((half, RANK, SHARE), F32),
            V((RINGS, 2, RANK, SHARE), BF),
            V((RINGS, 2, RANK, SHARE), BF),
            V((2, RANK, SHARE), F32),
            V((RANK, SHARE), F32),
            V((HALF, COLS), F32),
            V((HALF, COLS), F32),
            V((COLS, 8), F32),
            dma((7,)),
            dma((len(FWD_PIECES),)),
            dma((len(FWD_PIECES),)),
            dma((GRAD_PIECES,)),
            dma((GRAD_PIECES,)),
            dma((4,)),
            dma((4,)),
            dma((3,)),
            dma((3,)),
            dma((21,)),
            dma((21,)),
            dma((3,)),
            dma((3,)),
            dma((3,)),
            dma((3,)),
            pltpu.SemaphoreType.REGULAR((7,)),
        ],
        compiler_params=pltpu.CompilerParams(
            collective_id=0, has_side_effects=True, vmem_limit_bytes=40 * 2**20
        ),
        name="relay_tick",
    )(
        *[
            pltpu.with_memory_space_constraint(value, pltpu.HBM)
            for value in (
                section_out[0], saved_stream[0], section_grad[0], key_grad[0],
                key_weight[0], adapter_in[0].T, adapter_out[0], magnitude,
            )
        ]
    )
    keys, so, mg, og, ig = hand_over(keys, so, mg, og, ig)
    return (keys[None], so[None], mg, og.T[None], ig.T[None])


def solution(mesh):
    placed = (
        P("pipe", "dp", "tensor"),
        P("pipe", "dp", "tensor"),
        P("pipe", "dp", "tensor"),
        P("pipe", ("dp", "tensor"), None),
        P("pipe", "tensor", None),
        P("pipe", "tensor", None),
        P("pipe", None, None),
        P("pipe", None),
    )
    return jax.shard_map(
        per_device,
        mesh=mesh,
        in_specs=placed,
        out_specs=(
            P("pipe", ("dp", "tensor"), None),
            P("pipe", "dp", "tensor"),
            P("pipe", None),
            P("pipe", None, "dp"),
            P("pipe", ("tensor", "dp"), None),
        ),
        check_vma=False,
    )
```

```python
import jax
import jax.numpy as jnp
from jax import lax
from jax.experimental import pallas as pl
from jax.experimental.pallas import tpu as pltpu
from jax.sharding import PartitionSpec as P

EPSILON = 1e-06
MESH = pl.DeviceIdType.MESH
BF = jnp.bfloat16
F32 = jnp.float32

PIPES = 4
REPLICAS = 32
HUB = 2
RINGS = 8
TOK = 128
HALF = 64
COLS = 512
RANK = 64
FEAT = 8192
SHARE = FEAT // REPLICAS
OUTROWS = COLS // REPLICAS
DEPTH = 1024
STREAM = 2048
FWD_PIECES = (
    (False, 0, 4096),
    (False, 4096, 4096),
    (True, 0, 4096),
    (True, 4096, 2048),
    (True, 6144, 1024),
    (True, 7168, 1024),
)
GRAD_PIECES = 8
GRAD_ROWS = TOK // GRAD_PIECES


def mm(left, right, left_dim, right_dim):
    return lax.dot_general(
        left, right, (((left_dim,), (right_dim,)), ((), ())), preferred_element_type=F32
    )


def halves(value):
    upper = value.astype(BF)
    lower = (value - upper.astype(F32)).astype(BF)
    return upper, lower


def mm2(wide, narrow, left_dim, right_dim):
    upper, lower = halves(wide)
    return mm(upper, narrow, left_dim, right_dim) + mm(lower, narrow, left_dim, right_dim)


def kernel(
    x, sv, sg, kg, w, bt, a_in, mag_in,
    keys, so, mg, og, ig,
    a, mag, wv, bv, lv, fw, gr, sp, kc, raw, low, sqs, ksb, lgv, fac, flo,
    ox, oxr, o2, o2r, o3, o3r, o4, o4r,
    s0, s0r, s1, s1r, zs, s3, s3r,
    im, io, ra, sb, rb, c0, rc, fp, fpr, cv,
    loc, fs, fr, gs, gf, ts, tr, cs, cr, zsd, zrv, hs, hr, qs, qr, know,
):
    p = lax.axis_index("pipe")
    d = lax.axis_index("dp")
    t = lax.axis_index("tensor")
    z, h, c = d // 4, (d // 2) % 2, d % 2

    def dev(p_=p, z_=z, h_=h, c_=c, t_=t):
        return {"pipe": p_, "dp": (z_ * 2 + h_) * 2 + c_, "tensor": t_}

    up, down = dev(p_=(p + 1) % PIPES), dev(p_=(p + PIPES - 1) % PIPES)
    pair, mate, across = dev(t_=1 - t), dev(c_=1 - c), dev(h_=1 - h)
    both_other = dev(t_=1 - t, c_=1 - c)
    ring = [dev(z_=(z + k) % RINGS) for k in range(1, RINGS)]

    def remote(src, dst, ssem, rsem, to):
        cp = pltpu.make_async_remote_copy(
            src_ref=src, dst_ref=dst, send_sem=ssem, recv_sem=rsem, device_id=to, device_id_type=MESH
        )
        cp.start()
        return cp

    def signal(sem, to):
        pl.semaphore_signal(sem, inc=1, device_id=to, device_id_type=MESH)

    def meet(sem, step):
        @pl.when(z >= step)
        def _():
            signal(sem, dev(z_=z - step))

        @pl.when(z + step < RINGS)
        def _():
            signal(sem, dev(z_=z + step))

    def met(step):
        return jnp.where(z >= step, 1, 0) + jnp.where(z + step < RINGS, 1, 0)

    barrier = pltpu.get_barrier_semaphore()
    near = [up, down, mate]
    hub, hub_mate = (p == HUB) & (c == 0), (p == HUB) & (c == 1)
    below, ends = p == HUB - 1, (p == HUB + 1) | (p == HUB - 2)
    for to in near:
        signal(barrier, to)

    @pl.when(hub)
    def _():
        signal(barrier, pair)
        signal(barrier, across)
        meet(barrier, 1)

    mine = pl.ds(pl.multiple_of(c * (FEAT // 2), FEAT // 2), FEAT // 2)
    others = pl.ds(pl.multiple_of((1 - c) * (FEAT // 2), FEAT // 2), FEAT // 2)
    first = [
        pltpu.make_async_copy(a_in, a, loc.at[0]),
        pltpu.make_async_copy(mag_in, mag, loc.at[1]),
        pltpu.make_async_copy(bt, bv, loc.at[2]),
        pltpu.make_async_copy(w.at[mine], wv.at[mine], loc.at[3]),
    ]
    second = [
        pltpu.make_async_copy(kg, kc.at[t], loc.at[4]),
        pltpu.make_async_copy(sv, lv, loc.at[5]),
        pltpu.make_async_copy(w.at[others], wv.at[others], loc.at[6]),
    ]
    for cp in first + second:
        cp.start()

    pl.semaphore_wait(barrier, len(near) + jnp.where(hub, 2 + met(1), 0))

    fwd, grad = [], []
    for i in range(GRAD_PIECES):
        if i < len(FWD_PIECES):
            own, start, width = FWD_PIECES[i]
            rows = pl.ds(pl.multiple_of((t if own else 1 - t) * HALF, HALF), HALF)
            at = (rows, pl.ds(start, width))
            fwd.append(remote(x.at[at], fw.at[at], fs.at[i], fr.at[i], up))
        at = pl.ds(i * GRAD_ROWS, GRAD_ROWS)
        grad.append(remote(sg.at[at], gr.at[at], gs.at[i], gf.at[i], down))

    @pl.when(below)
    def _():
        signal(know.at[0], up)

    @pl.when(hub_mate)
    def _():
        pl.semaphore_wait(know.at[0], 1)
        signal(know.at[0], mate)

    @pl.when(hub)
    def _():
        pl.semaphore_wait(know.at[0], 2)
        signal(know.at[5], pair)
        signal(know.at[1], across)
        meet(know.at[1], 1)
        pl.semaphore_wait(know.at[5], 1)
        for to in near:
            signal(know.at[6], to)

    here = t * 2 + c
    sqs[here] = jnp.zeros((8, COLS), F32)
    for cp in first:
        cp.wait()
    av = a[...]

    @pl.when(hub_mate)
    def _():
        pl.semaphore_wait(know.at[6], 1)
        signal(know.at[6], up)
        signal(know.at[6], down)

    @pl.when(hub)
    def _():
        pl.semaphore_wait(know.at[1], 1 + met(1))
        meet(know.at[2], 2)

    @pl.loop(0, FEAT // 2 // DEPTH)
    def _(i):
        part = pl.ds(pl.multiple_of(c * (FEAT // 2) + i * DEPTH, DEPTH), DEPTH)
        combined = wv[part, :].astype(F32) + mm(bv[:, part], a[...], 0, 0)
        sqs[here] += jnp.sum((combined * combined).reshape(DEPTH // 8, 8, COLS), axis=0)

    @pl.when(below)
    def _():
        pl.semaphore_wait(know.at[6], 1)
        signal(know.at[6], down)

    @pl.when(hub)
    def _():
        pl.semaphore_wait(know.at[2], met(2))
        meet(know.at[3], 4)

    raw[...] = jnp.zeros_like(raw)
    low[...] = jnp.zeros_like(low)
    for cp in second:
        cp.wait()

    def saved_piece(i):
        part = pl.ds(pl.multiple_of(i * DEPTH, DEPTH), DEPTH)
        left = lv[:, part]
        raw[...] += mm(left, wv[part, :], 1, 0)
        low[...] += mm(left, bv[:, part], 1, 1)

    pl.loop(0, FEAT // DEPTH // 2)(saved_piece)

    @pl.when(ends)
    def _():
        pl.semaphore_wait(know.at[6], 1)

    kcp = remote(kg, kc.at[t], ts.at[0], tr.at[0], pair)
    sqc = [
        remote(sqs.at[here], sqs.at[here], qs.at[k], qr.at[k], to)
        for k, to in enumerate([pair, mate, both_other])
    ]

    pl.loop(FEAT // DEPTH // 2, FEAT // DEPTH)(saved_piece)

    kcp.wait_recv()
    cot = kc[...].reshape(TOK, COLS)
    for cp in sqc:
        cp.wait_recv()
    norm = jnp.sqrt(
        jnp.sum((sqs[0] + sqs[1]) + (sqs[2] + sqs[3]), axis=0, keepdims=True) + EPSILON
    )
    scale = mag[...] / norm
    shi, slo = halves(cot.astype(F32) * scale)
    ksb[...] = shi
    low_grad = mm(shi, av, 1, 1) + mm(slo, av, 1, 1)
    lgv[...] = low_grad.astype(BF)
    turned_grad = low_grad.T.astype(BF)

    def token_sum(i, core):
        part = pl.ds(pl.multiple_of((i * 2 + core) * SHARE, SHARE), SHARE)
        return mm(turned_grad, lv[:, part], 1, 0)

    @pl.loop(0, REPLICAS // 2)
    def _(i):
        im[i] = token_sum(i, 1 - c)

    imc = remote(im, ra, cs.at[0], cr.at[0], mate)

    @pl.when(hub)
    def _():
        pl.semaphore_wait(know.at[3], met(4))
        for to in near:
            signal(know.at[4], to)

    lhi, llo = halves(low[...])
    raw_saved = raw[...] + mm(lhi, av, 1, 0) + mm(llo, av, 1, 0)
    s0[...] = jnp.sum((cot.astype(F32) * raw_saved).reshape(TOK // 8, 8, COLS), axis=0)
    s0c = remote(s0, s0r, ts.at[1], tr.at[1], pair)
    part = pl.ds(pl.multiple_of(d * SHARE, SHARE), SHARE)
    b_share = bv[:, part]
    cross = mm(b_share, wv[part, :], 1, 0) + mm2(mm(b_share, b_share, 1, 1), av, 1, 0)
    ox[:, pl.ds(0, RANK)] = mm(cot, lhi, 0, 0) + mm(cot, llo, 0, 0)
    ox[:, pl.ds(RANK, RANK)] = cross.T
    oxc = remote(ox, oxr, ts.at[2], tr.at[2], pair)

    @pl.when(hub_mate)
    def _():
        pl.semaphore_wait(know.at[4], 1)
        signal(know.at[4], up)
        signal(know.at[4], down)

    @pl.loop(0, REPLICAS // 2)
    def _(i):
        io[i] = token_sum(i, c)

    @pl.when(below)
    def _():
        pl.semaphore_wait(know.at[4], 1)
        signal(know.at[4], down)

    s0c.wait_recv()
    s1[...] = s0[...] + s0r[...]
    s1c = remote(s1, s1r, cs.at[1], cr.at[1], mate)

    imc.wait_recv()

    @pl.when(ends)
    def _():
        pl.semaphore_wait(know.at[4], 1)

    @pl.loop(0, RINGS)
    def _(i):
        for k in range(2):
            sb[i, k] = (io[i * 2 + k] + ra[i * 2 + k]).astype(BF)

    sbc = [
        remote(sb.at[(z + k + 1) % RINGS], rb.at[z], zsd.at[14 + k], zrv.at[14 + k], to)
        for k, to in enumerate(ring)
    ]

    oxc.wait_recv()
    sums = (ox[...] + oxr[...]).reshape(REPLICAS // 2, 2, OUTROWS, 2 * RANK)
    o2[0] = sums[:, 0]
    o2[1] = sums[:, 1]
    o2c = remote(o2.at[1 - c], o2r, cs.at[2], cr.at[2], mate)

    def stream_piece(i):
        part = pl.ds(pl.multiple_of(i * STREAM, STREAM), STREAM)
        sp[:, part] = mm(ksb[...], wv[part, :], 1, 1) + mm(lgv[...], bv[:, part], 1, 0)

    pl.loop(0, FEAT // STREAM // 2)(stream_piece)

    s1c.wait_recv()
    zs[z] = s1[...] + s1r[...]
    zsc = [remote(zs.at[z], zs.at[z], zsd.at[k], zrv.at[k], to) for k, to in enumerate(ring)]
    o2c.wait_recv()
    o3[...] = (o2[c] + o2r[...]).reshape(RINGS, 2, OUTROWS, 2 * RANK)
    o3c = [
        remote(o3.at[(z + k + 1) % RINGS], o3r.at[z], zsd.at[7 + k], zrv.at[7 + k], to)
        for k, to in enumerate(ring)
    ]

    pl.loop(FEAT // STREAM // 2, FEAT // STREAM)(stream_piece)

    def finish_grad(i):
        grad[i].wait_recv()
        at = pl.ds(i * GRAD_ROWS, GRAD_ROWS)
        so[at] = (sp[at] + gr[at].astype(F32)).astype(BF)

    def take_forward(i):
        fwd[i].wait_recv()
        own, start, width = FWD_PIECES[i]
        rows = pl.ds(pl.multiple_of((t if own else 1 - t) * HALF, HALF), HALF)
        if start == 0:
            fac[...] = jnp.zeros_like(fac)
            flo[...] = jnp.zeros_like(flo)

        depth = min(width, DEPTH)

        @pl.loop(0, width // depth)
        def _(k):
            part = pl.ds(pl.multiple_of(start + k * depth, depth), depth)
            rowsv = fw[rows, part]
            fac[...] += mm(rowsv, wv[part, :], 1, 0)
            flo[...] += mm(rowsv, bv[:, part], 1, 1)

    def partial_keys():
        return fac[...] + mm2(flo[...], a[...], 1, 0)

    take_forward(0)
    finish_grad(0)
    take_forward(1)
    finish_grad(1)
    finish_grad(2)
    finish_grad(3)
    fp[...] = partial_keys()
    fpc = remote(fp, fpr, ts.at[3], tr.at[3], pair)

    for cp in zsc:
        cp.wait_recv()
    total = zs[0]
    for k in range(1, RINGS):
        total = total + zs[k]
    s3[...] = total
    s3c = remote(s3, s3r, hs.at[0], hr.at[0], across)
    for cp in o3c:
        cp.wait_recv()
    total = o3[z]
    for k in range(1, RINGS):
        total = total + o3r[(z + k) % RINGS]
    o4[...] = total
    o4c = remote(o4.at[1 - h], o4r, hs.at[1], hr.at[1], across)

    for cp in sbc:
        cp.wait_recv()
    for k in range(2):
        total = io[z * 2 + k] + ra[z * 2 + k]
        for n in range(1, RINGS):
            total = total + rb[(z + n) % RINGS, k].astype(F32)
        c0[k] = total
    c0c = remote(c0.at[1 - h], rc, hs.at[2], hr.at[2], across)

    take_forward(2)
    finish_grad(4)
    s3c.wait_recv()
    scale_grad = jnp.sum(s3[...] + s3r[...], axis=0, keepdims=True)
    factor = -scale_grad * mag[...] / (norm * norm * norm)
    mg[...] = scale_grad / norm / REPLICAS
    columns = jnp.concatenate([scale, factor, jnp.zeros((6, COLS), F32)], axis=0)
    cv[...] = columns.T
    o4c.wait_recv()
    lines = pl.ds(pl.multiple_of(d * OUTROWS, OUTROWS), OUTROWS)
    whole = o4[h] + o4r[...]
    og[...] = (
        whole[:, :RANK] * cv[lines, pl.ds(0, 1)] + whole[:, RANK:] * cv[lines, pl.ds(1, 1)]
    ) / REPLICAS
    turned = a[...].astype(F32) * factor
    thi, tlo = halves(turned)
    part = pl.ds(pl.multiple_of(d * SHARE, SHARE), SHARE)
    wsh = wv[part, :]
    small = mm(thi, a[...], 1, 1) + mm(tlo, a[...], 1, 1)
    term = mm(thi, wsh, 1, 1) + mm(tlo, wsh, 1, 1) + mm2(small, bv[:, part], 1, 0)

    finish_grad(5)
    take_forward(3)
    c0c.wait_recv()
    ig[...] = (c0[h] + rc[...] + term) / REPLICAS
    fpc.wait_recv()
    finish_grad(6)
    take_forward(4)
    for cp in [kcp, s0c, oxc, imc, s1c, o2c, fpc, s3c, o4c, c0c] + sqc + zsc + o3c + sbc + fwd[:4] + grad[:6]:
        cp.wait_send()
    take_forward(5)
    keys[...] = ((partial_keys() + fpr[...]) * scale).astype(BF)
    finish_grad(7)

    for cp in fwd[4:] + grad[6:]:
        cp.wait_send()


def hand_over(*results):
    count = len(results)
    places = []
    for i, value in enumerate(results):
        rows = value.shape[0]
        cuts = 2 if rows == TOK else 1
        places += [(i, pl.ds(k * (rows // cuts), rows // cuts)) for k in range(cuts)]
    places.sort(key=lambda place: -results[place[0]].size)

    def copies(*refs):
        moves = [
            pltpu.make_async_copy(refs[i].at[at], refs[count + i].at[at], refs[-1].at[k])
            for k, (i, at) in enumerate(places)
        ]
        for cp in moves:
            cp.start()
        for cp in moves:
            cp.wait()

    return pl.pallas_call(
        copies,
        out_shape=[jax.ShapeDtypeStruct(r.shape, r.dtype) for r in results],
        in_specs=[pl.BlockSpec(memory_space=pl.ANY)] * count,
        out_specs=[pl.BlockSpec(memory_space=pl.ANY)] * count,
        scratch_shapes=[pltpu.SemaphoreType.DMA((len(places),))],
        compiler_params=pltpu.CompilerParams(vmem_limit_bytes=2**20),
        name="hand_over",
    )(*results)


def per_device(section_out, saved_stream, section_grad, key_grad, key_weight, adapter_in, adapter_out, magnitude):
    vmem = pl.BlockSpec(memory_space=pltpu.VMEM)
    hbm = pl.BlockSpec(memory_space=pl.ANY)
    dma = pltpu.SemaphoreType.DMA
    V = pltpu.VMEM
    half = REPLICAS // 2
    keys, so, mg, og, ig = pl.pallas_call(
        kernel,
        out_shape=[
            V((HALF, COLS), BF),
            V((TOK, FEAT), BF),
            V((1, COLS), F32),
            V((OUTROWS, RANK), F32),
            V((RANK, SHARE), F32),
        ],
        in_specs=[hbm] * 8,
        out_specs=[vmem] * 5,
        scratch_shapes=[
            V((RANK, COLS), BF),
            V((1, COLS), F32),
            V((FEAT, COLS), BF),
            V((RANK, FEAT), BF),
            V((TOK, FEAT), BF),
            V((TOK, FEAT), BF),
            V((TOK, FEAT), BF),
            V((TOK, FEAT), F32),
            V((2, HALF, COLS), BF),
            V((TOK, COLS), F32),
            V((TOK, RANK), F32),
            V((4, 8, COLS), F32),
            V((TOK, COLS), BF),
            V((TOK, RANK), BF),
            V((HALF, COLS), F32),
            V((HALF, RANK), F32),
            V((COLS, 2 * RANK), F32),
            V((COLS, 2 * RANK), F32),
            V((2, half, OUTROWS, 2 * RANK), F32),
            V((half, OUTROWS, 2 * RANK), F32),
            V((RINGS, 2, OUTROWS, 2 * RANK), F32),
            V((RINGS, 2, OUTROWS, 2 * RANK), F32),
            V((2, OUTROWS, 2 * RANK), F32),
            V((OUTROWS, 2 * RANK), F32),
            V((8, COLS), F32),
            V((8, COLS), F32),
            V((8, COLS), F32),
            V((8, COLS), F32),
            V((RINGS, 8, COLS), F32),
            V((8, COLS), F32),
            V((8, COLS), F32),
            V((half, RANK, SHARE), F32),
            V((half, RANK, SHARE), F32),
            V((half, RANK, SHARE), F32),
            V((RINGS, 2, RANK, SHARE), BF),
            V((RINGS, 2, RANK, SHARE), BF),
            V((2, RANK, SHARE), F32),
            V((RANK, SHARE), F32),
            V((HALF, COLS), F32),
            V((HALF, COLS), F32),
            V((COLS, 8), F32),
            dma((7,)),
            dma((len(FWD_PIECES),)),
            dma((len(FWD_PIECES),)),
            dma((GRAD_PIECES,)),
            dma((GRAD_PIECES,)),
            dma((4,)),
            dma((4,)),
            dma((3,)),
            dma((3,)),
            dma((21,)),
            dma((21,)),
            dma((3,)),
            dma((3,)),
            dma((3,)),
            dma((3,)),
            pltpu.SemaphoreType.REGULAR((7,)),
        ],
        compiler_params=pltpu.CompilerParams(
            collective_id=0, has_side_effects=True, vmem_limit_bytes=40 * 2**20
        ),
        name="relay_tick",
    )(
        *[
            pltpu.with_memory_space_constraint(value, pltpu.HBM)
            for value in (
                section_out[0], saved_stream[0], section_grad[0], key_grad[0],
                key_weight[0], adapter_in[0].T, adapter_out[0], magnitude,
            )
        ]
    )
    keys, so, mg, og, ig = hand_over(keys, so, mg, og, ig)
    return (keys[None], so[None], mg, og.T[None], ig.T[None])


def solution(mesh):
    placed = (
        P("pipe", "dp", "tensor"),
        P("pipe", "dp", "tensor"),
        P("pipe", "dp", "tensor"),
        P("pipe", ("dp", "tensor"), None),
        P("pipe", "tensor", None),
        P("pipe", "tensor", None),
        P("pipe", None, None),
        P("pipe", None),
    )
    return jax.shard_map(
        per_device,
        mesh=mesh,
        in_specs=placed,
        out_specs=(
            P("pipe", ("dp", "tensor"), None),
            P("pipe", "dp", "tensor"),
            P("pipe", None),
            P("pipe", None, "dp"),
            P("pipe", ("tensor", "dp"), None),
        ),
        check_vma=False,
    )
```

```python
import jax
import jax.numpy as jnp
from jax import lax
from jax.experimental import pallas as pl
from jax.experimental.pallas import tpu as pltpu
from jax.sharding import PartitionSpec as P

EPSILON = 1e-06
MESH = pl.DeviceIdType.MESH
BF = jnp.bfloat16
F32 = jnp.float32

PIPES = 4
REPLICAS = 32
HUB = 2
RINGS = 8
TOK = 128
HALF = 64
COLS = 512
RANK = 64
FEAT = 8192
SHARE = FEAT // REPLICAS
OUTROWS = COLS // REPLICAS
DEPTH = 1024
STREAM = 2048
FWD_PIECES = (
    (False, 0, 4096),
    (False, 4096, 4096),
    (True, 0, 4096),
    (True, 4096, 3072),
    (True, 7168, 512),
    (True, 7680, 512),
)
GRAD_PIECES = 8
GRAD_ROWS = TOK // GRAD_PIECES


def mm(left, right, left_dim, right_dim):
    return lax.dot_general(
        left, right, (((left_dim,), (right_dim,)), ((), ())), preferred_element_type=F32
    )


def halves(value):
    upper = value.astype(BF)
    lower = (value - upper.astype(F32)).astype(BF)
    return upper, lower


def mm2(wide, narrow, left_dim, right_dim):
    upper, lower = halves(wide)
    return mm(upper, narrow, left_dim, right_dim) + mm(lower, narrow, left_dim, right_dim)


def kernel(
    x, sv, sg, kg, w, bt, a_in, mag_in,
    keys, so, mg, og, ig,
    a, mag, wv, bv, lv, fw, gr, sp, kc, raw, low, sqs, ksb, lgv, fac, flo,
    ox, oxr, o2, o2r, o3, o3r, o4, o4r,
    s0, s0r, s1, s1r, zs, s3, s3r,
    im, io, ra, sb, rb, c0, rc, fp, fpr, cv,
    loc, fs, fr, gs, gf, ts, tr, cs, cr, zsd, zrv, hs, hr, qs, qr, know,
):
    p = lax.axis_index("pipe")
    d = lax.axis_index("dp")
    t = lax.axis_index("tensor")
    z, h, c = d // 4, (d // 2) % 2, d % 2

    def dev(p_=p, z_=z, h_=h, c_=c, t_=t):
        return {"pipe": p_, "dp": (z_ * 2 + h_) * 2 + c_, "tensor": t_}

    up, down = dev(p_=(p + 1) % PIPES), dev(p_=(p + PIPES - 1) % PIPES)
    pair, mate, across = dev(t_=1 - t), dev(c_=1 - c), dev(h_=1 - h)
    both_other = dev(t_=1 - t, c_=1 - c)
    ring = [dev(z_=(z + k) % RINGS) for k in range(1, RINGS)]

    def remote(src, dst, ssem, rsem, to):
        cp = pltpu.make_async_remote_copy(
            src_ref=src, dst_ref=dst, send_sem=ssem, recv_sem=rsem, device_id=to, device_id_type=MESH
        )
        cp.start()
        return cp

    def signal(sem, to):
        pl.semaphore_signal(sem, inc=1, device_id=to, device_id_type=MESH)

    def meet(sem, step):
        @pl.when(z >= step)
        def _():
            signal(sem, dev(z_=z - step))

        @pl.when(z + step < RINGS)
        def _():
            signal(sem, dev(z_=z + step))

    def met(step):
        return jnp.where(z >= step, 1, 0) + jnp.where(z + step < RINGS, 1, 0)

    barrier = pltpu.get_barrier_semaphore()
    near = [up, down, mate]
    hub, hub_mate = (p == HUB) & (c == 0), (p == HUB) & (c == 1)
    below, ends = p == HUB - 1, (p == HUB + 1) | (p == HUB - 2)
    for to in near:
        signal(barrier, to)

    @pl.when(hub)
    def _():
        signal(barrier, pair)
        signal(barrier, across)
        meet(barrier, 1)

    mine = pl.ds(pl.multiple_of(c * (FEAT // 2), FEAT // 2), FEAT // 2)
    others = pl.ds(pl.multiple_of((1 - c) * (FEAT // 2), FEAT // 2), FEAT // 2)
    first = [
        pltpu.make_async_copy(a_in, a, loc.at[0]),
        pltpu.make_async_copy(mag_in, mag, loc.at[1]),
        pltpu.make_async_copy(bt, bv, loc.at[2]),
        pltpu.make_async_copy(w.at[mine], wv.at[mine], loc.at[3]),
    ]
    second = [
        pltpu.make_async_copy(kg, kc.at[t], loc.at[4]),
        pltpu.make_async_copy(sv, lv, loc.at[5]),
        pltpu.make_async_copy(w.at[others], wv.at[others], loc.at[6]),
    ]
    for cp in first + second:
        cp.start()

    pl.semaphore_wait(barrier, len(near) + jnp.where(hub, 2 + met(1), 0))

    fwd, grad = [], []
    for i in range(GRAD_PIECES):
        if i < len(FWD_PIECES):
            own, start, width = FWD_PIECES[i]
            rows = pl.ds(pl.multiple_of((t if own else 1 - t) * HALF, HALF), HALF)
            at = (rows, pl.ds(start, width))
            fwd.append(remote(x.at[at], fw.at[at], fs.at[i], fr.at[i], up))
        at = pl.ds(i * GRAD_ROWS, GRAD_ROWS)
        grad.append(remote(sg.at[at], gr.at[at], gs.at[i], gf.at[i], down))

    @pl.when(below)
    def _():
        signal(know.at[0], up)

    @pl.when(hub_mate)
    def _():
        pl.semaphore_wait(know.at[0], 1)
        signal(know.at[0], mate)

    @pl.when(hub)
    def _():
        pl.semaphore_wait(know.at[0], 2)
        signal(know.at[5], pair)
        signal(know.at[1], across)
        meet(know.at[1], 1)
        pl.semaphore_wait(know.at[5], 1)
        for to in near:
            signal(know.at[6], to)

    here = t * 2 + c
    sqs[here] = jnp.zeros((8, COLS), F32)
    for cp in first:
        cp.wait()
    av = a[...]

    @pl.when(hub_mate)
    def _():
        pl.semaphore_wait(know.at[6], 1)
        signal(know.at[6], up)
        signal(know.at[6], down)

    @pl.when(hub)
    def _():
        pl.semaphore_wait(know.at[1], 1 + met(1))
        meet(know.at[2], 2)

    @pl.loop(0, FEAT // 2 // DEPTH)
    def _(i):
        part = pl.ds(pl.multiple_of(c * (FEAT // 2) + i * DEPTH, DEPTH), DEPTH)
        combined = wv[part, :].astype(F32) + mm(bv[:, part], a[...], 0, 0)
        sqs[here] += jnp.sum((combined * combined).reshape(DEPTH // 8, 8, COLS), axis=0)

    @pl.when(below)
    def _():
        pl.semaphore_wait(know.at[6], 1)
        signal(know.at[6], down)

    @pl.when(hub)
    def _():
        pl.semaphore_wait(know.at[2], met(2))
        meet(know.at[3], 4)

    raw[...] = jnp.zeros_like(raw)
    low[...] = jnp.zeros_like(low)
    for cp in second:
        cp.wait()

    def saved_piece(i):
        part = pl.ds(pl.multiple_of(i * DEPTH, DEPTH), DEPTH)
        left = lv[:, part]
        raw[...] += mm(left, wv[part, :], 1, 0)
        low[...] += mm(left, bv[:, part], 1, 1)

    pl.loop(0, FEAT // DEPTH // 2)(saved_piece)

    @pl.when(ends)
    def _():
        pl.semaphore_wait(know.at[6], 1)

    kcp = remote(kg, kc.at[t], ts.at[0], tr.at[0], pair)
    sqc = [
        remote(sqs.at[here], sqs.at[here], qs.at[k], qr.at[k], to)
        for k, to in enumerate([pair, mate, both_other])
    ]

    pl.loop(FEAT // DEPTH // 2, FEAT // DEPTH)(saved_piece)

    kcp.wait_recv()
    cot = kc[...].reshape(TOK, COLS)
    for cp in sqc:
        cp.wait_recv()
    norm = jnp.sqrt(
        jnp.sum((sqs[0] + sqs[1]) + (sqs[2] + sqs[3]), axis=0, keepdims=True) + EPSILON
    )
    scale = mag[...] / norm
    shi, slo = halves(cot.astype(F32) * scale)
    ksb[...] = shi
    low_grad = mm(shi, av, 1, 1) + mm(slo, av, 1, 1)
    lgv[...] = low_grad.astype(BF)
    turned_grad = low_grad.T.astype(BF)

    def token_sum(i, core):
        part = pl.ds(pl.multiple_of((i * 2 + core) * SHARE, SHARE), SHARE)
        return mm(turned_grad, lv[:, part], 1, 0)

    @pl.loop(0, REPLICAS // 2)
    def _(i):
        im[i] = token_sum(i, 1 - c)

    imc = remote(im, ra, cs.at[0], cr.at[0], mate)

    @pl.when(hub)
    def _():
        pl.semaphore_wait(know.at[3], met(4))
        for to in near:
            signal(know.at[4], to)

    lhi, llo = halves(low[...])
    raw_saved = raw[...] + mm(lhi, av, 1, 0) + mm(llo, av, 1, 0)
    s0[...] = jnp.sum((cot.astype(F32) * raw_saved).reshape(TOK // 8, 8, COLS), axis=0)
    s0c = remote(s0, s0r, ts.at[1], tr.at[1], pair)
    part = pl.ds(pl.multiple_of(d * SHARE, SHARE), SHARE)
    b_share = bv[:, part]
    cross = mm(b_share, wv[part, :], 1, 0) + mm2(mm(b_share, b_share, 1, 1), av, 1, 0)
    ox[:, pl.ds(0, RANK)] = mm(cot, lhi, 0, 0) + mm(cot, llo, 0, 0)
    ox[:, pl.ds(RANK, RANK)] = cross.T
    oxc = remote(ox, oxr, ts.at[2], tr.at[2], pair)

    @pl.when(hub_mate)
    def _():
        pl.semaphore_wait(know.at[4], 1)
        signal(know.at[4], up)
        signal(know.at[4], down)

    @pl.loop(0, REPLICAS // 2)
    def _(i):
        io[i] = token_sum(i, c)

    @pl.when(below)
    def _():
        pl.semaphore_wait(know.at[4], 1)
        signal(know.at[4], down)

    s0c.wait_recv()
    s1[...] = s0[...] + s0r[...]
    s1c = remote(s1, s1r, cs.at[1], cr.at[1], mate)

    imc.wait_recv()

    @pl.when(ends)
    def _():
        pl.semaphore_wait(know.at[4], 1)

    @pl.loop(0, RINGS)
    def _(i):
        for k in range(2):
            sb[i, k] = (io[i * 2 + k] + ra[i * 2 + k]).astype(BF)

    sbc = [
        remote(sb.at[(z + k + 1) % RINGS], rb.at[z], zsd.at[14 + k], zrv.at[14 + k], to)
        for k, to in enumerate(ring)
    ]

    oxc.wait_recv()
    sums = (ox[...] + oxr[...]).reshape(REPLICAS // 2, 2, OUTROWS, 2 * RANK)
    o2[0] = sums[:, 0]
    o2[1] = sums[:, 1]
    o2c = remote(o2.at[1 - c], o2r, cs.at[2], cr.at[2], mate)

    def stream_piece(i):
        part = pl.ds(pl.multiple_of(i * STREAM, STREAM), STREAM)
        sp[:, part] = mm(ksb[...], wv[part, :], 1, 1) + mm(lgv[...], bv[:, part], 1, 0)

    pl.loop(0, FEAT // STREAM // 2)(stream_piece)

    s1c.wait_recv()
    zs[z] = s1[...] + s1r[...]
    zsc = [remote(zs.at[z], zs.at[z], zsd.at[k], zrv.at[k], to) for k, to in enumerate(ring)]
    o2c.wait_recv()
    o3[...] = (o2[c] + o2r[...]).reshape(RINGS, 2, OUTROWS, 2 * RANK)
    o3c = [
        remote(o3.at[(z + k + 1) % RINGS], o3r.at[z], zsd.at[7 + k], zrv.at[7 + k], to)
        for k, to in enumerate(ring)
    ]

    pl.loop(FEAT // STREAM // 2, FEAT // STREAM)(stream_piece)

    def finish_grad(i):
        grad[i].wait_recv()
        at = pl.ds(i * GRAD_ROWS, GRAD_ROWS)
        so[at] = (sp[at] + gr[at].astype(F32)).astype(BF)

    def take_forward(i):
        fwd[i].wait_recv()
        own, start, width = FWD_PIECES[i]
        rows = pl.ds(pl.multiple_of((t if own else 1 - t) * HALF, HALF), HALF)
        if start == 0:
            fac[...] = jnp.zeros_like(fac)
            flo[...] = jnp.zeros_like(flo)

        depth = min(width, DEPTH)

        @pl.loop(0, width // depth)
        def _(k):
            part = pl.ds(pl.multiple_of(start + k * depth, depth), depth)
            rowsv = fw[rows, part]
            fac[...] += mm(rowsv, wv[part, :], 1, 0)
            flo[...] += mm(rowsv, bv[:, part], 1, 1)

    def partial_keys():
        return fac[...] + mm2(flo[...], a[...], 1, 0)

    take_forward(0)
    finish_grad(0)
    take_forward(1)
    finish_grad(1)
    finish_grad(2)
    finish_grad(3)
    fp[...] = partial_keys()
    fpc = remote(fp, fpr, ts.at[3], tr.at[3], pair)

    for cp in zsc:
        cp.wait_recv()
    total = zs[0]
    for k in range(1, RINGS):
        total = total + zs[k]
    s3[...] = total
    s3c = remote(s3, s3r, hs.at[0], hr.at[0], across)
    for cp in o3c:
        cp.wait_recv()
    total = o3[z]
    for k in range(1, RINGS):
        total = total + o3r[(z + k) % RINGS]
    o4[...] = total
    o4c = remote(o4.at[1 - h], o4r, hs.at[1], hr.at[1], across)

    for cp in sbc:
        cp.wait_recv()
    for k in range(2):
        total = io[z * 2 + k] + ra[z * 2 + k]
        for n in range(1, RINGS):
            total = total + rb[(z + n) % RINGS, k].astype(F32)
        c0[k] = total
    c0c = remote(c0.at[1 - h], rc, hs.at[2], hr.at[2], across)

    take_forward(2)
    finish_grad(4)
    s3c.wait_recv()
    scale_grad = jnp.sum(s3[...] + s3r[...], axis=0, keepdims=True)
    factor = -scale_grad * mag[...] / (norm * norm * norm)
    mg[...] = scale_grad / norm / REPLICAS
    columns = jnp.concatenate([scale, factor, jnp.zeros((6, COLS), F32)], axis=0)
    cv[...] = columns.T
    o4c.wait_recv()
    lines = pl.ds(pl.multiple_of(d * OUTROWS, OUTROWS), OUTROWS)
    whole = o4[h] + o4r[...]
    og[...] = (
        whole[:, :RANK] * cv[lines, pl.ds(0, 1)] + whole[:, RANK:] * cv[lines, pl.ds(1, 1)]
    ) / REPLICAS
    turned = a[...].astype(F32) * factor
    thi, tlo = halves(turned)
    part = pl.ds(pl.multiple_of(d * SHARE, SHARE), SHARE)
    wsh = wv[part, :]
    small = mm(thi, a[...], 1, 1) + mm(tlo, a[...], 1, 1)
    term = mm(thi, wsh, 1, 1) + mm(tlo, wsh, 1, 1) + mm2(small, bv[:, part], 1, 0)

    finish_grad(5)
    take_forward(3)
    c0c.wait_recv()
    ig[...] = (c0[h] + rc[...] + term) / REPLICAS
    fpc.wait_recv()
    finish_grad(6)
    take_forward(4)
    for cp in [kcp, s0c, oxc, imc, s1c, o2c, fpc, s3c, o4c, c0c] + sqc + zsc + o3c + sbc + fwd[:4] + grad[:6]:
        cp.wait_send()
    take_forward(5)
    keys[...] = ((partial_keys() + fpr[...]) * scale).astype(BF)
    finish_grad(7)

    for cp in fwd[4:] + grad[6:]:
        cp.wait_send()


def hand_over(*results):
    count = len(results)
    places = []
    for i, value in enumerate(results):
        rows = value.shape[0]
        cuts = 2 if rows == TOK else 1
        places += [(i, pl.ds(k * (rows // cuts), rows // cuts)) for k in range(cuts)]
    places.sort(key=lambda place: -results[place[0]].size)

    def copies(*refs):
        moves = [
            pltpu.make_async_copy(refs[i].at[at], refs[count + i].at[at], refs[-1].at[k])
            for k, (i, at) in enumerate(places)
        ]
        for cp in moves:
            cp.start()
        for cp in moves:
            cp.wait()

    return pl.pallas_call(
        copies,
        out_shape=[jax.ShapeDtypeStruct(r.shape, r.dtype) for r in results],
        in_specs=[pl.BlockSpec(memory_space=pl.ANY)] * count,
        out_specs=[pl.BlockSpec(memory_space=pl.ANY)] * count,
        scratch_shapes=[pltpu.SemaphoreType.DMA((len(places),))],
        compiler_params=pltpu.CompilerParams(vmem_limit_bytes=2**20),
        name="hand_over",
    )(*results)


def per_device(section_out, saved_stream, section_grad, key_grad, key_weight, adapter_in, adapter_out, magnitude):
    vmem = pl.BlockSpec(memory_space=pltpu.VMEM)
    hbm = pl.BlockSpec(memory_space=pl.ANY)
    dma = pltpu.SemaphoreType.DMA
    V = pltpu.VMEM
    half = REPLICAS // 2
    keys, so, mg, og, ig = pl.pallas_call(
        kernel,
        out_shape=[
            V((HALF, COLS), BF),
            V((TOK, FEAT), BF),
            V((1, COLS), F32),
            V((OUTROWS, RANK), F32),
            V((RANK, SHARE), F32),
        ],
        in_specs=[hbm] * 8,
        out_specs=[vmem] * 5,
        scratch_shapes=[
            V((RANK, COLS), BF),
            V((1, COLS), F32),
            V((FEAT, COLS), BF),
            V((RANK, FEAT), BF),
            V((TOK, FEAT), BF),
            V((TOK, FEAT), BF),
            V((TOK, FEAT), BF),
            V((TOK, FEAT), F32),
            V((2, HALF, COLS), BF),
            V((TOK, COLS), F32),
            V((TOK, RANK), F32),
            V((4, 8, COLS), F32),
            V((TOK, COLS), BF),
            V((TOK, RANK), BF),
            V((HALF, COLS), F32),
            V((HALF, RANK), F32),
            V((COLS, 2 * RANK), F32),
            V((COLS, 2 * RANK), F32),
            V((2, half, OUTROWS, 2 * RANK), F32),
            V((half, OUTROWS, 2 * RANK), F32),
            V((RINGS, 2, OUTROWS, 2 * RANK), F32),
            V((RINGS, 2, OUTROWS, 2 * RANK), F32),
            V((2, OUTROWS, 2 * RANK), F32),
            V((OUTROWS, 2 * RANK), F32),
            V((8, COLS), F32),
            V((8, COLS), F32),
            V((8, COLS), F32),
            V((8, COLS), F32),
            V((RINGS, 8, COLS), F32),
            V((8, COLS), F32),
            V((8, COLS), F32),
            V((half, RANK, SHARE), F32),
            V((half, RANK, SHARE), F32),
            V((half, RANK, SHARE), F32),
            V((RINGS, 2, RANK, SHARE), BF),
            V((RINGS, 2, RANK, SHARE), BF),
            V((2, RANK, SHARE), F32),
            V((RANK, SHARE), F32),
            V((HALF, COLS), F32),
            V((HALF, COLS), F32),
            V((COLS, 8), F32),
            dma((7,)),
            dma((len(FWD_PIECES),)),
            dma((len(FWD_PIECES),)),
            dma((GRAD_PIECES,)),
            dma((GRAD_PIECES,)),
            dma((4,)),
            dma((4,)),
            dma((3,)),
            dma((3,)),
            dma((21,)),
            dma((21,)),
            dma((3,)),
            dma((3,)),
            dma((3,)),
            dma((3,)),
            pltpu.SemaphoreType.REGULAR((7,)),
        ],
        compiler_params=pltpu.CompilerParams(
            collective_id=0, has_side_effects=True, vmem_limit_bytes=40 * 2**20
        ),
        name="relay_tick",
    )(
        *[
            pltpu.with_memory_space_constraint(value, pltpu.HBM)
            for value in (
                section_out[0], saved_stream[0], section_grad[0], key_grad[0],
                key_weight[0], adapter_in[0].T, adapter_out[0], magnitude,
            )
        ]
    )
    keys, so, mg, og, ig = hand_over(keys, so, mg, og, ig)
    return (keys[None], so[None], mg, og.T[None], ig.T[None])


def solution(mesh):
    placed = (
        P("pipe", "dp", "tensor"),
        P("pipe", "dp", "tensor"),
        P("pipe", "dp", "tensor"),
        P("pipe", ("dp", "tensor"), None),
        P("pipe", "tensor", None),
        P("pipe", "tensor", None),
        P("pipe", None, None),
        P("pipe", None),
    )
    return jax.shard_map(
        per_device,
        mesh=mesh,
        in_specs=placed,
        out_specs=(
            P("pipe", ("dp", "tensor"), None),
            P("pipe", "dp", "tensor"),
            P("pipe", None),
            P("pipe", None, "dp"),
            P("pipe", ("tensor", "dp"), None),
        ),
        check_vma=False,
    )
```
